512 devices in a mesh: dp: 64 (over y_lo, z, core), fsdp: 8 (over x, y_hi).
Axes of the slice: x: 4, y: 4 (y_hi: 2, y_lo: 2; y = y_hi * 2 + y_lo), z: 16, core: 2. Of those that a mesh axis runs over, the one named last changes fastest.
Arguments:
- tokens: bfloat16 [262144, 1024], P(('dp', 'fsdp')), may hold values from -6 to 6
- w_in: bfloat16 [1024, 2048], P('fsdp'), may hold values from -0.1875 to 0.1875
- b_in: float32 [2048], replicated, may hold values from -3 to 3
- w_out: bfloat16 [2048, 1024], P('fsdp'), may hold values from -0.125 to 0.125
- b_out: float32 [1024], replicated, may hold values from -2 to 2
- ln_gain: float32 [1024], replicated, may hold values from 0.5 to 1.5
- ln_bias: float32 [1024], replicated, may hold values from -1.5 to 1.5
- head: bfloat16 [1024, 1024], replicated, may hold values from -0.1875 to 0.1875
- query_feats: bfloat16 [2048, 1024], P(('dp', 'fsdp')), may hold values from -6 to 6
- positive_rows: bfloat16 [2048, 1024], P(('dp', 'fsdp')), may hold values from -1 to 1
- neg_ids: int32 [2048, 64], P(('dp', 'fsdp')), may hold values from 0 to 2047, as said below
Outputs:
- refreshed: bfloat16 [2048, 1024], P(('dp', 'fsdp'))
- loss: float32 [2048], P(('dp', 'fsdp'))
- head_grad: float32 [1024, 1024], P('fsdp')
The draws below stay inside these ranges and needn't reach their ends.
Inputs may be any that keep to these rules, and one draw needn't show every extreme that they name: `neg_ids`: in each aligned block of 4 queries (the queries of one device), ids in one range [g * 32, (g + 1) * 32) appear at most 16 times among the block's entries, and some range exactly 16 times.
All inputs are finite; a program needn't handle non-finite values.
Results may differ from the reference program's by a relative error of at most 0.012.
The reference program's roundings to bfloat16 on the way (of `hidden`, `query`, `neg_rows`, `weights` and `dquery`) count: a program that leaves them out, or rounds other values in their place, can miss the bound.
Values may be sent and summed in bfloat16 or wider, within the bound.
A program may use at most 64 MiB of HBM per device.

```python
import math
import jax
import jax.numpy as jnp
from jax import lax

D = 1024
FF = 2048
SEQ = 128
NEG = 64
Q_DEV = 4
GROUP = 32
PASSAGES = 2048
QUERIES = 2048
CAP = 16
N_FSDP = 8


def draw_neg_ids(key, part):
    key = jax.random.fold_in(key, 7)
    groups = PASSAGES // GROUP
    blocks = QUERIES // Q_DEV
    count = Q_DEV * NEG
    key_hot, key_shift, key_order, key_local = jax.random.split(key, 4)
    hot = jax.random.randint(key_hot, (), 0, groups)
    shift = jax.random.randint(key_shift, (blocks, 1), 0, groups - 1)
    slot = jnp.arange(count)[None, :]
    other = (hot + 1 + (slot - CAP + shift) % (groups - 1)) % groups
    owner = jnp.where(slot < CAP, hot, other)
    owner = jnp.broadcast_to(owner, (blocks, count))
    order = jax.vmap(lambda k: jax.random.permutation(k, count))(jax.random.split(key_order, blocks))
    owner = jnp.take_along_axis(owner, order, axis=1)
    local = jax.random.randint(key_local, (blocks, count), 0, GROUP)
    return (owner * GROUP + local).reshape(QUERIES, NEG).astype(jnp.int32)


def draw_tokens(key, part):
    key = jax.random.fold_in(key, 11)
    key_noise, key_pass, key_tok, key_dir, key_off = jax.random.split(key, 5)
    passage_scale = jnp.exp(jax.random.uniform(key_pass, (PASSAGES, 1, 1), jnp.float32, math.log(0.3), math.log(1.5)))
    token_scale = jnp.exp(jax.random.uniform(key_tok, (PASSAGES, SEQ, 1), jnp.float32, math.log(0.5), math.log(2.0)))
    direction = jax.random.normal(key_dir, (PASSAGES, 1, D), jnp.float32)
    noise = jax.random.normal(key_noise, (PASSAGES, SEQ, D), jnp.float32)
    offset = jax.random.uniform(key_off, (PASSAGES, 1, 1), jnp.float32, -1.0, 1.0)
    shifted = offset * direction
    values = passage_scale * token_scale * noise + shifted
    values = jnp.clip(values, -6.0, 6.0)
    return values.reshape(PASSAGES * SEQ, D).astype(jnp.bfloat16)


def draw_w_out(key, part):
    key = jax.random.fold_in(key, 13)
    key_base = jax.random.fold_in(key, 0)
    scale = 1.0 / math.sqrt(FF)
    values = scale * jax.random.normal(key_base, (FF, D), jnp.float32)
    values = jnp.clip(values, -0.125, 0.125)
    return values.astype(jnp.bfloat16)


def block_levels(rng, dims, pieces, least, high):
    level = 1.0
    for position, shards_of in pieces:
        heights = jax.random.uniform(jax.random.fold_in(jax.random.fold_in(rng, 6), position), (shards_of,), jnp.float32, least / len(pieces), high / len(pieces))
        level = level * jnp.repeat(jnp.exp(heights), dims[position] // shards_of).reshape((-1,) + (1,) * (len(dims) - 1 - position))
    return level


def scatter_about(key, extent, width, most, shards=(), dtype=jnp.bfloat16):
    gain = block_levels(key, extent, shards, -0.22, 0.18) if shards else 1.0
    array = jax.random.normal(key, extent, jnp.float32) * width * gain
    return jnp.minimum(jnp.maximum(array, -most), most).astype(dtype)


def setup_inputs(seed: int = 0) -> dict:
    key_of = jax.random.split(jax.random.key(seed), 12)
    return {
        "tokens": draw_tokens(jax.random.fold_in(key_of[11], 71), 0),
        "w_in": scatter_about(key_of[1], (D, FF), D ** -0.5, 0.1875, ((0, 8),)),
        "b_in": scatter_about(key_of[2], (FF,), 0.5, 3.0, (), jnp.float32),
        "w_out": draw_w_out(jax.random.fold_in(key_of[11], 71), 0),
        "b_out": scatter_about(key_of[4], (D,), 0.3, 2.0, (), jnp.float32),
        "ln_gain": jnp.clip(1.0 + 0.1 * jax.random.normal(key_of[5], (D,), jnp.float32), 0.5, 1.5),
        "ln_bias": scatter_about(key_of[6], (D,), 0.2, 1.5, (), jnp.float32),
        "head": scatter_about(key_of[7], (D, D), D ** -0.5, 0.1875),
        "query_feats": scatter_about(key_of[8], (QUERIES, D), 1.0, 6.0, ((0, 512),)),
        "positive_rows": scatter_about(key_of[9], (QUERIES, D), 0.15, 1.0, ((0, 512),)),
        "neg_ids": draw_neg_ids(jax.random.fold_in(key_of[11], 71), 0),
    }


score_scale = 0.5
eps = 1e-05

def encode_group(block, w_in, b_in, w_out, b_out, ln_gain, ln_bias):
    pre = jnp.dot(block, w_in, preferred_element_type=jnp.float32) + b_in
    hidden = jax.nn.gelu(pre, approximate=True).astype(jnp.bfloat16)
    summed = block.astype(jnp.float32) + jnp.dot(hidden, w_out, preferred_element_type=jnp.float32) + b_out
    center = summed - lax.optimization_barrier(jnp.mean(summed, axis=-1, keepdims=True))
    spread = lax.optimization_barrier(jnp.mean(center * center, axis=-1, keepdims=True))
    normed = center * lax.rsqrt(spread + eps) * ln_gain + ln_bias
    return lax.optimization_barrier(jnp.mean(normed.reshape(-1, SEQ, D), axis=1)).astype(jnp.bfloat16)

def reference(tokens, w_in, b_in, w_out, b_out, ln_gain, ln_bias, head, query_feats, positive_rows, neg_ids):
    blocks = tokens.reshape(PASSAGES // GROUP, GROUP * SEQ, D)
    refreshed = lax.map(lambda blk: encode_group(blk, w_in, b_in, w_out, b_out, ln_gain, ln_bias), blocks)
    refreshed = refreshed.reshape(PASSAGES, D)
    batches = QUERIES // (Q_DEV * N_FSDP)

    def step(carry, inputs):
        feats, positive, ids = inputs
        query = jnp.dot(feats, head, preferred_element_type=jnp.float32).astype(jnp.bfloat16)
        neg_rows = jnp.take(refreshed, ids, axis=0)
        qf = query.astype(jnp.float32)
        s_neg = score_scale * jnp.einsum('qd,qkd->qk', qf, neg_rows.astype(jnp.float32))
        s_pos = score_scale * lax.optimization_barrier(jnp.sum(qf * positive.astype(jnp.float32), axis=-1))
        top = jnp.maximum(s_pos, lax.optimization_barrier(jnp.max(s_neg, axis=-1)))
        total = top + jnp.log(jnp.exp(s_pos - top) + lax.optimization_barrier(jnp.sum(jnp.exp(s_neg - top[:, None]), axis=-1)))
        loss = total - s_pos
        weights = jnp.exp(s_neg - total[:, None]).astype(jnp.bfloat16)
        mixed = jnp.einsum('qk,qkd->qd', weights.astype(jnp.float32), neg_rows.astype(jnp.float32))
        coeff = jnp.exp(s_pos - total) - 1.0
        dquery = (score_scale * (coeff[:, None] * positive.astype(jnp.float32) + mixed)).astype(jnp.bfloat16)
        term = jnp.einsum('qa,qb->ab', feats.astype(jnp.float32), dquery.astype(jnp.float32))
        return (carry + term, loss)
    inputs = (query_feats.reshape(batches, -1, D), positive_rows.reshape(batches, -1, D), neg_ids.reshape(batches, -1, NEG))
    head_grad, losses = lax.scan(step, jnp.zeros((D, D), jnp.float32), inputs)
    return (refreshed, losses.reshape(QUERIES), head_grad)
```

```python
import jax
import jax.numpy as jnp
from jax import lax
from jax.experimental import pallas as pl
from jax.experimental.pallas import tpu as pltpu
from jax.sharding import PartitionSpec as P

SEQ = 128
NX, NZ, NF, NPLANE = 4, 16, 8, 32
score_scale = 0.5
eps = 1e-05
LOW = -3.0e38
MESH = pl.DeviceIdType.MESH
F32, BF16 = jnp.float32, jnp.bfloat16


def iota(shape, dim):
    return lax.broadcasted_iota(jnp.int32, shape, dim)


def dot(a, b, dims=(1, 0)):
    return lax.dot_general(
        a, b, (((dims[0],), (dims[1],)), ((), ())), preferred_element_type=F32
    )


def pick(mask):
    return mask.astype(F32).astype(BF16)


def take_all(ref, sem):
    pltpu.make_async_copy(ref, ref, sem).wait()


def kernel(
    tok, win, b_in, wout, b_out, gain, bias, head, feats, pos, ids,
    emb, loss, hg,
    W1, W2, hid, summed, stg, qf16, idsb, pos16, r16, qfs, qfr, query, queryf, posf, idst, cT, rk,
    stb, wr, gr, rss, rsr, agr,
    xl, xr, fl, fr, orv, srv, sa, sb, ssend, loc,
    zq, zi, pp, fq, rp, zs, fw, gx, zr, za, ga, psend,
):
    dp, f = lax.axis_index("dp"), lax.axis_index("fsdp")
    yl, z, c = dp // 32, (dp // 2) % NZ, dp % 2
    x, yh = f // 2, f % 2
    k = yl * 2 + c
    d = k * NF + f

    def chip(xx, hh, ll, cc):
        return (ll * 32 + z * 2 + cc, xx * 2 + hh)

    right, left = chip((x + 1) % NX, yh, yl, c), chip((x + 3) % NX, yh, yl, c)
    other, same = chip(x, 1 - yh, 1 - yl, c), chip(x, yh, 1 - yl, c)
    sibling = chip(x, yh, yl, 1 - c)

    def plane_peer(i):
        e = (d + i) % NPLANE
        return ((e // 16) * 32 + z * 2 + (e // 8) % 2, e % NF)

    def z_at(n):
        away = NZ // 2 + ((n + 1) // 2) * (2 * (n % 2) - 1)
        return (z + away) % NZ

    def z_peer(zz):
        return (yl * 32 + zz * 2 + c, f)

    def f_at(i):
        return (f + i) % NF

    def quarter_peer(i):
        e = (k + i) % 4
        return ((e // 2) * 32 + z * 2 + e % 2, f)

    def send(src, dst, ss, rs, to):
        copy = pltpu.make_async_remote_copy(
            src_ref=src, dst_ref=dst, send_sem=ss, recv_sem=rs, device_id=to, device_id_type=MESH
        )
        copy.start()
        return copy

    barrier = pltpu.get_barrier_semaphore()

    @pl.loop(1, NPLANE)
    def _(i):
        pl.semaphore_signal(barrier, inc=1, device_id=plane_peer(i), device_id_type=MESH)

    @pl.loop(0, NZ - 1)
    def _(n):
        pl.semaphore_signal(barrier, inc=1, device_id=z_peer(z_at(n)), device_id_type=MESH)

    def spread(rows):
        for i in range(4):
            for j in range(4):
                stg[pl.ds(i * 4 + j, 1), :] = rows[i : i + 1, j * 256 : (j + 1) * 256]
        return stg[...].astype(BF16)

    qf16[z] = spread(feats[...].astype(F32))
    pos16[d] = spread(pos[...].astype(F32))
    posf[...] = jnp.zeros_like(posf)
    posf[0:4, :] = pos[...].astype(F32)
    idsb[z] = jnp.full((8, 128), -1, jnp.int32)
    idsb[z, 0:4, 0:64] = ids[...]

    pl.semaphore_wait(barrier, NPLANE - 1 + NZ - 1)

    def stage(s):
        if s < 2:
            return win, W1, pl.ds(s * 1024, 1024)
        return wout, W2, pl.ds((s - 2) * 512, 512)

    sent = []

    def out(s, n, src, dst, rs, to):
        sent.append(send(src, dst, ssend.at[s, n], rs, to))

    def landed(ref, sem):
        take_all(ref, sem)

    def own(s):
        shard, W, cols = stage(s)
        src = shard.at[c, :, :, cols]
        dst = W.at[x, yh, c, :, :, cols]
        out(s, 0, src, dst, xl.at[s], right)
        out(s, 1, src, dst, xr.at[s], left)
        out(s, 2, shard.at[c, 1 - yl, :, cols], W.at[x, yh, c, 1 - yl, :, cols], orv.at[s], other)

    xm, xp, xo = (x + 3) % NX, (x + 1) % NX, (x + 2) % NX

    def first(s):
        _, W, cols = stage(s)
        landed(W.at[xm, yh, c, :, :, cols], xl.at[s])
        out(s, 3, W.at[xm, yh, c, 0, :, cols], W.at[xm, yh, c, 0, :, cols], fl.at[s], right)
        half = W.at[xm, yh, c, 1 - yl, :, cols]
        out(s, 4, half, half, orv.at[s], other)
        landed(W.at[xp, yh, c, :, :, cols], xr.at[s])
        out(s, 5, W.at[xp, yh, c, 1, :, cols], W.at[xp, yh, c, 1, :, cols], fr.at[s], left)
        half = W.at[xp, yh, c, 1 - yl, :, cols]
        out(s, 6, half, half, orv.at[s], other)

    def second(s):
        _, W, cols = stage(s)
        landed(W.at[xo, yh, c, 0, :, cols], fl.at[s])
        landed(W.at[xo, yh, c, 1, :, cols], fr.at[s])
        half = W.at[xo, yh, c, 1 - yl, :, cols]
        out(s, 7, half, half, orv.at[s], other)
        mine = W.at[:, yh, c, :, :, cols]
        out(s, 8, mine, mine, sa.at[s], sibling)

    def third(s):
        _, W, cols = stage(s)
        theirs = W.at[:, 1 - yh, c, yl, :, cols]
        landed(theirs, orv.at[s])
        out(s, 9, theirs, theirs, srv.at[s], same)

    def fourth(s):
        _, W, cols = stage(s)
        landed(W.at[:, 1 - yh, c, 1 - yl, :, cols], srv.at[s])
        theirs = W.at[:, 1 - yh, c, :, :, cols]
        out(s, 10, theirs, theirs, sb.at[s], sibling)

    def whole(s):
        _, W, cols = stage(s)
        landed(W.at[:, yh, 1 - c, :, :, cols], sa.at[s])
        landed(W.at[:, 1 - yh, 1 - c, :, :, cols], sb.at[s])

    def compute(s):
        if s < 2:

            @pl.loop(0, 4)
            def _(n):
                at = pl.ds(pl.multiple_of(s * 1024 + n * 256, 256), 256)
                w = W1[:, :, :, :, :, at].reshape(1024, 256)
                v = dot(tok[...], w) + b_in[:, at]
                g = 0.5 * v * (1.0 + jnp.tanh(0.7978845608 * (v + 0.044715 * (v * v * v))))
                hid[:, at] = g.astype(BF16)
        else:

            @pl.loop(0, 2)
            def _(n):
                at = pl.ds(pl.multiple_of((s - 2) * 512 + n * 256, 256), 256)
                w = W2[:, :, :, :, :, at].reshape(2048, 256)
                summed[:, at] = tok[:, at].astype(F32) + dot(hid[...], w) + b_out[:, at]

    own(0)
    own(1)
    keep1 = pltpu.make_async_copy(win.at[c], W1.at[x, yh, c], loc.at[0])
    keep2 = pltpu.make_async_copy(wout.at[c], W2.at[x, yh, c], loc.at[1])
    keep1.start()
    keep2.start()

    @pl.loop(0, NZ - 1)
    def _(n):
        to = z_peer(z_at(n))
        send(qf16.at[z], qf16.at[z], psend.at[0], zq.at[0], to)
        send(idsb.at[z], idsb.at[z], psend.at[1], zi.at[0], to)

    keep1.wait()
    keep2.wait()

    first(0)
    own(2)
    second(0)
    first(1)
    own(3)

    take_all(qf16.at[pl.ds(0, NZ - 1)], zq.at[0])
    flat = qf16[...].reshape(NZ * 16, 256)
    for j in range(4):
        sel = pick(iota((64, 256), 1) == 4 * iota((64, 256), 0) + j)
        rows = dot(sel, flat).astype(BF16)
        qfs[2 * j] = rows[:, :128]
        qfs[2 * j + 1] = rows[:, 128:]
    qfr[f] = qfs[f]

    @pl.loop(1, NF)
    def _(i):
        to = f_at(i)
        send(qfs.at[to], qfr.at[f], psend.at[2], fq.at[0], (dp, to))

    third(0)
    second(1)
    first(2)

    @pl.loop(1, NPLANE)
    def _(i):
        send(pos16.at[d], pos16.at[d], psend.at[3], pp.at[0], plane_peer(i))

    fourth(0)
    third(1)
    second(2)

    total_q = jnp.zeros((128, 1024), F32)
    m = iota((128, 256), 0)
    for j in range(4):
        sel = pick((iota((128, 256), 1) == (m // 8) * 16 + (m % 8) * 4 + j) & (m % 8 < 4))
        rows = dot(sel, flat).astype(BF16)
        total_q = total_q + dot(rows, head[j * 256 : (j + 1) * 256, :])
    query[...] = total_q.astype(BF16)
    queryf[...] = query[...].astype(F32)

    first(3)
    whole(0)
    compute(0)
    fourth(1)
    third(2)
    second(3)

    take_all(idsb.at[pl.ds(0, NZ - 1)], zi.at[0])
    idst[...] = jnp.transpose(idsb[...].reshape(128, 128).astype(F32))
    pi = iota((128, 1), 0)
    pid = (((pi // 64) * 32 + z * 2 + (pi // 32) % 2) * NF + (pi // 4) % NF) * 4 + pi % 4
    pid = pid.astype(F32)
    cT[...] = lax.fori_loop(
        0, 64,
        lambda t, a: a + (idst[pl.ds(t, 1), :] == pid).astype(F32),
        jnp.zeros((128, 128), F32),
    )

    third(3)
    whole(1)
    compute(1)
    fourth(2)
    fourth(3)
    whole(2)
    compute(2)
    whole(3)
    compute(3)

    rows = []
    for i in range(4):
        v = summed[i * SEQ : (i + 1) * SEQ, :]
        center = v - jnp.mean(v, axis=-1, keepdims=True)
        spread_ = jnp.mean(center * center, axis=-1, keepdims=True)
        normed = center * lax.rsqrt(spread_ + eps)
        rows.append(jnp.sum(normed, axis=0, keepdims=True) * (1.0 / SEQ) * gain[...] + bias[...])
    pooled = jnp.concatenate(rows, axis=0)
    emb[...] = pooled.astype(BF16)
    r16[d] = spread(pooled)

    @pl.loop(1, NPLANE)
    def _(i):
        send(r16.at[d], r16.at[d], psend.at[4], rp.at[0], plane_peer(i))

    lane = iota((1, 128), 1)
    mine = (lane // 8 == z) & (lane % 8 < 4)
    s_col = score_scale * jnp.sum(
        queryf[pl.ds(pl.multiple_of(z * 8, 8), 8), :] * posf[...], axis=-1, keepdims=True
    )
    s_pos = jnp.sum(
        jnp.where(iota((8, 128), 1) == z * 8 + iota((8, 128), 0), s_col, 0.0), axis=0, keepdims=True
    )

    take_all(r16.at[pl.ds(0, NPLANE - 1)], rp.at[0])
    flat_r = r16[...].reshape(NPLANE * 16, 256)
    s = jnp.zeros((128, 128), F32)
    for j in range(4):
        sel = pick(iota((128, 512), 1) == 4 * iota((128, 512), 0) + j)
        rows = dot(sel, flat_r).astype(BF16)
        rk[j] = rows
        s = s + dot(rows, query[:, j * 256 : (j + 1) * 256], (1, 1))
    s = s * score_scale
    count = cT[...]
    listed = count > 0.0
    high = jnp.max(jnp.where(listed, s, LOW), axis=0, keepdims=True)
    part = jnp.sum(
        jnp.where(listed, count * jnp.exp(jnp.where(listed, s - high, 0.0)), 0.0), axis=0, keepdims=True
    )
    high2 = jnp.where(mine, jnp.maximum(high, s_pos), high)
    part2 = part * jnp.exp(high - high2) + jnp.where(mine, jnp.exp(s_pos - high2), 0.0)
    r8 = iota((8, 128), 0)
    stb[z] = jnp.where(r8 == 0, high2, jnp.where(r8 == 1, part2, 0.0))

    @pl.loop(0, NZ - 1)
    def _(n):
        send(stb.at[z], stb.at[z], psend.at[5], zs.at[0], z_peer(z_at(n)))

    take_all(stb.at[pl.ds(0, NZ - 1)], zs.at[0])
    stats = stb[...]
    highs, parts = stats[:, 0, :], stats[:, 1, :]
    top = jnp.max(highs, axis=0, keepdims=True)
    total = top + jnp.log(jnp.sum(parts * jnp.exp(highs - top), axis=0, keepdims=True))
    loss[...] = jnp.where(r8 == 0, jnp.where(mine, total - s_pos, 0.0), 0.0)
    coeff = jnp.where(mine, jnp.exp(jnp.where(mine, s_pos - total, 0.0)) - 1.0, 0.0)
    w = jnp.exp(jnp.where(listed, s - total, 0.0)).astype(BF16).astype(F32)
    w = jnp.where(listed, count * w, 0.0).astype(BF16)
    j64 = iota((64, 128), 0)
    wr[f, 0:64, :] = dot(pick(iota((64, 128), 1) == (j64 // 4) * 8 + j64 % 4), w, (1, 1)).astype(BF16)
    c0 = coeff.astype(BF16).astype(F32)
    c1 = (coeff - c0).astype(BF16).astype(F32)
    c2 = coeff - c0 - c1
    r16i = iota((16, 128), 0)
    wr[f, 64:80, :] = jnp.where(
        r16i == 0, c0, jnp.where(r16i == 1, c1, jnp.where(r16i == 2, c2, 0.0))
    ).astype(BF16)

    @pl.loop(1, NF)
    def _(i):
        send(wr.at[f], wr.at[f], psend.at[6], fw.at[0], (dp, f_at(i)))

    take_all(pos16.at[pl.ds(0, NPLANE - 1)], pp.at[0])
    sel = pick(iota((128, 512), 1) == 4 * iota((128, 512), 0) + k)
    pos_k = dot(sel, pos16[...].reshape(NPLANE * 16, 256)).astype(BF16)
    take_all(qfr.at[pl.ds(0, NF - 1)], fq.at[0])
    slices = qfr[...].reshape(NF * 64, 128)
    g32 = iota((32, 512), 0)
    group_q = dot(pick(iota((32, 512), 1) == (g32 // 4) * 64 + z * 4 + g32 % 4), slices)

    take_all(wr.at[pl.ds(0, NF - 1)], fw.at[0])
    g_part = dot(wr[:, 0:64, :].reshape(NF * 64, 128), slices, (0, 0))
    e32, l32 = iota((32, 128), 0), iota((32, 128), 1)
    expand = pick((l32 // 16 == e32 // 4) & (l32 % 16 < 3))
    co = dot(expand, wr[:, 64:80, :].reshape(128, 128))
    co = jnp.sum(jnp.where(l32 == z * 8 + e32 % 4, co, 0.0), axis=1, keepdims=True)
    gr[k, 0:128, :] = g_part.astype(BF16)
    gr[k, 128:160, :] = (group_q * co).astype(BF16)

    @pl.loop(1, 4)
    def _(i):
        send(gr.at[k], gr.at[k], psend.at[7], gx.at[0], quarter_peer(i))

    take_all(gr.at[pl.ds(0, 3)], gx.at[0])
    g_all = gr[...]
    g_sum = jnp.sum(g_all[:, 0:128, :].astype(F32), axis=0).astype(BF16)
    g_pos = g_all[:, 128:160, :].reshape(128, 128)
    term = score_scale * (dot(g_sum, rk[k], (0, 0)) + dot(g_pos, pos_k, (0, 0)))
    for t in range(NZ):
        rss[t] = term[(t // 2) * 16 : (t // 2) * 16 + 16, (t % 2) * 128 : (t % 2) * 128 + 128]
    rsr[z] = rss[z]

    @pl.loop(0, NZ - 1)
    def _(n):
        to = z_at(n)
        send(rss.at[to], rsr.at[z], psend.at[8], zr.at[0], z_peer(to))

    take_all(rsr.at[pl.ds(0, NZ - 1)], zr.at[0])
    agr[k, z] = jnp.sum(rsr[...], axis=0).astype(BF16)

    @pl.loop(0, NZ - 1)
    def _(n):
        send(agr.at[k, z], agr.at[k, z], psend.at[9], za.at[0], z_peer(z_at(n)))

    take_all(agr.at[k, pl.ds(0, NZ - 1)], za.at[0])

    @pl.loop(1, 4)
    def _(i):
        send(agr.at[k], agr.at[k], psend.at[10], ga.at[0], quarter_peer(i))

    take_all(agr.at[pl.ds(0, 3)], ga.at[0])
    for e in range(4):
        for t in range(NZ):
            at = e * 256 + (t % 2) * 128
            hg[(t // 2) * 16 : (t // 2) * 16 + 16, at : at + 128] = agr[e, t].astype(F32)

    for copy in sent:
        copy.wait_send()
    take_all(qf16.at[pl.ds(0, NZ - 1)], psend.at[0])
    take_all(idsb.at[pl.ds(0, NZ - 1)], psend.at[1])
    take_all(qfr.at[pl.ds(0, NF - 1)], psend.at[2])
    take_all(pos16.at[pl.ds(0, NPLANE - 1)], psend.at[3])
    take_all(r16.at[pl.ds(0, NPLANE - 1)], psend.at[4])
    take_all(stb.at[pl.ds(0, NZ - 1)], psend.at[5])
    take_all(wr.at[pl.ds(0, NF - 1)], psend.at[6])
    take_all(gr.at[pl.ds(0, 3)], psend.at[7])
    take_all(rsr.at[pl.ds(0, NZ - 1)], psend.at[8])
    take_all(agr.at[0, pl.ds(0, NZ - 1)], psend.at[9])
    take_all(agr.at[pl.ds(0, 3)], psend.at[10])


def body(
    tokens, w_in, b_in, w_out, b_out, ln_gain, ln_bias, head, query_feats, positive_rows, neg_ids
):
    vmem = pl.BlockSpec(memory_space=pltpu.VMEM)
    V, S = pltpu.VMEM, pltpu.SemaphoreType.DMA
    embedded, loss, head_grad = pl.pallas_call(
        kernel,
        out_shape=(
            jax.ShapeDtypeStruct((4, 1024), BF16),
            jax.ShapeDtypeStruct((8, 128), F32),
            jax.ShapeDtypeStruct((128, 1024), F32),
        ),
        in_specs=[vmem] * 11,
        out_specs=(vmem,) * 3,
        scratch_shapes=[
            V((4, 2, 2, 2, 32, 2048), BF16),
            V((4, 2, 2, 2, 64, 1024), BF16),
            V((512, 2048), BF16),
            V((512, 1024), F32),
            V((16, 256), F32),
            V((NZ, 16, 256), BF16),
            V((NZ, 8, 128), jnp.int32),
            V((NPLANE, 16, 256), BF16),
            V((NPLANE, 16, 256), BF16),
            V((NF, 64, 128), BF16),
            V((NF, 64, 128), BF16),
            V((128, 1024), BF16),
            V((128, 1024), F32),
            V((8, 1024), F32),
            V((128, 128), F32),
            V((128, 128), F32),
            V((4, 128, 256), BF16),
            V((NZ, 8, 128), F32),
            V((NF, 80, 128), BF16),
            V((4, 160, 128), BF16),
            V((NZ, 16, 128), F32),
            V((NZ, 16, 128), F32),
            V((4, NZ, 16, 128), BF16),
        ]
        + [S((4,))] * 8
        + [S((4, 11)), S((2,))]
        + [S((1,))] * 11
        + [S((11,))],
        compiler_params=pltpu.CompilerParams(
            collective_id=0, has_side_effects=True, vmem_limit_bytes=48 << 20
        ),
    )(
        tokens,
        w_in.reshape(2, 2, 32, 2048),
        b_in.reshape(1, -1),
        w_out.reshape(2, 2, 64, 1024),
        b_out.reshape(1, -1),
        ln_gain.reshape(1, -1),
        ln_bias.reshape(1, -1),
        head,
        query_feats,
        positive_rows,
        neg_ids,
    )
    z = (lax.axis_index("dp") // 2) % NZ
    return embedded, lax.dynamic_slice_in_dim(loss[0], z * 8, 4), head_grad


def solution(mesh):
    in_specs = (
        P(("dp", "fsdp"), None),
        P("fsdp", None),
        P(),
        P("fsdp", None),
        P(),
        P(),
        P(),
        P(),
        P(("dp", "fsdp"), None),
        P(("dp", "fsdp"), None),
        P(("dp", "fsdp"), None),
    )
    out_specs = (P(("dp", "fsdp"), None), P(("dp", "fsdp")), P("fsdp", None))
    return jax.shard_map(body, mesh=mesh, in_specs=in_specs, out_specs=out_specs, check_vma=False)
```

```python
import jax
import jax.numpy as jnp
from jax import lax
from jax.experimental import pallas as pl
from jax.experimental.pallas import tpu as pltpu
from jax.sharding import PartitionSpec as P

SEQ = 128
NX, NZ, NF, NPLANE = 4, 16, 8, 32
S1, S2 = 2, 2
score_scale = 0.5
eps = 1e-05
LOW = -3.0e38
MESH = pl.DeviceIdType.MESH
F32, BF16 = jnp.float32, jnp.bfloat16


def iota(shape, dim):
    return lax.broadcasted_iota(jnp.int32, shape, dim)


def dot(a, b, dims=(1, 0)):
    return lax.dot_general(
        a, b, (((dims[0],), (dims[1],)), ((), ())), preferred_element_type=F32
    )


def pick(mask):
    return mask.astype(F32).astype(BF16)


def take_all(ref, sem):
    pltpu.make_async_copy(ref, ref, sem).wait()


def kernel(
    tok_h, win, b_in_h, wout, b_out_h, gain_h, bias_h, head_h, feats_h, pos_h, ids_h,
    emb, loss, hg,
    tok, b_in, b_out, gain, bias, head, feats, pos, ids, inp,
    W1, W2, hid, summed, stg, qf16, idsb, pos16, r16, qfs, qfr, query, queryf, posf, idst, cT, rk,
    pk, stb, wr, gs, gr, rss, rsr, agr,
    crv, irv, srv, ssend, loc,
    zq, zi, pp, fq, rp, zs, fw, gx, zr, za, ga, psend,
):
    dp, f = lax.axis_index("dp"), lax.axis_index("fsdp")
    yl, z, c = dp // 32, (dp // 2) % NZ, dp % 2
    x, yh = f // 2, f % 2
    k = yl * 2 + c
    d = k * NF + f

    def chip(xx, hh, ll, cc):
        return (ll * 32 + z * 2 + cc, xx * 2 + hh)

    right, left = chip((x + 1) % NX, yh, yl, c), chip((x + 3) % NX, yh, yl, c)
    other, same = chip(x, 1 - yh, 1 - yl, c), chip(x, yh, 1 - yl, c)
    sibling = chip(x, yh, yl, 1 - c)

    def plane_peer(i):
        e = (d + i) % NPLANE
        return ((e // 16) * 32 + z * 2 + (e // 8) % 2, e % NF)

    def z_at(n):
        away = NZ // 2 + ((n + 1) // 2) * (2 * (n % 2) - 1)
        return (z + away) % NZ

    def z_peer(zz):
        return (yl * 32 + zz * 2 + c, f)

    def f_at(i):
        return (f + i) % NF

    def quarter_peer(i):
        e = (k + i) % 4
        return ((e // 2) * 32 + z * 2 + e % 2, f)

    def send(src, dst, ss, rs, to):
        copy = pltpu.make_async_remote_copy(
            src_ref=src, dst_ref=dst, send_sem=ss, recv_sem=rs, device_id=to, device_id_type=MESH
        )
        copy.start()
        return copy

    fetched = [
        pltpu.make_async_copy(a, b, inp.at[i])
        for i, (a, b) in enumerate(
            [(feats_h, feats), (pos_h, pos), (ids_h, ids), (tok_h, tok), (head_h, head),
             (b_in_h, b_in), (b_out_h, b_out), (gain_h, gain), (bias_h, bias)]
        )
    ]
    for copy in fetched:
        copy.start()

    barrier = pltpu.get_barrier_semaphore()

    @pl.loop(1, NPLANE)
    def _(i):
        pl.semaphore_signal(barrier, inc=1, device_id=plane_peer(i), device_id_type=MESH)

    @pl.loop(0, NZ - 1)
    def _(n):
        pl.semaphore_signal(barrier, inc=1, device_id=z_peer(z_at(n)), device_id_type=MESH)

    def spread(rows):
        for i in range(4):
            for j in range(4):
                stg[pl.ds(i * 4 + j, 1), :] = rows[i : i + 1, j * 256 : (j + 1) * 256]
        return stg[...].astype(BF16)

    for copy in fetched[:3]:
        copy.wait()
    qf16[z] = spread(feats[...].astype(F32))
    pos16[d] = spread(pos[...].astype(F32))
    posf[...] = jnp.zeros_like(posf)
    posf[0:4, :] = pos[...].astype(F32)
    idsb[z] = jnp.full((8, 128), -1, jnp.int32)
    idsb[z, 0:4, 0:64] = ids[...]

    pl.semaphore_wait(barrier, NPLANE - 1 + NZ - 1)

    col = (z + yl + yh) % 2
    xm, xp, xo = (x + 3) % NX, (x + 1) % NX, (x + 2) % NX
    zp, zm = z_peer((z + 1) % NZ), z_peer((z + NZ - 1) % NZ)
    far = chip(xo, yh, yl, c)

    def stage(s):
        if s < S1:
            return win, W1, pl.ds(s * (2048 // S1), 2048 // S1)
        return wout, W2, pl.ds((s - S1) * (1024 // S2), 1024 // S2)

    sent, leaving = [], []

    def out(s, n, ref, rs, to, src=None):
        sent.append(send(ref if src is None else src, ref, ssend.at[s, n], rs, to))

    def part(s, xx, hh, half):
        _, W, cols = stage(s)
        return W.at[xx, hh, c, half, :, cols]

    def ago(s):
        shard, _, cols = stage(s)
        ref, src = part(s, x, yh, col), shard.at[c, col, :, cols]
        out(s, 0, ref, crv.at[s, 0], right, src)
        out(s, 1, ref, crv.at[s, 1], left, src)
        out(s, 2, ref, crv.at[s, 3], other, src)
        out(s, 3, ref, crv.at[s, 2], far, src)

    def bgo(s):
        ref = part(s, x, 1 - yh, col)
        take_all(ref, crv.at[s, 3])
        out(s, 4, ref, crv.at[s, 4], right)
        out(s, 5, ref, crv.at[s, 5], left)
        out(s, 6, ref, irv.at[s, 1], same)
        ref = part(s, xm, yh, col)
        take_all(ref, crv.at[s, 0])
        out(s, 7, ref, irv.at[s, 0], same)
        ref = part(s, xp, yh, col)
        take_all(ref, crv.at[s, 1])
        out(s, 8, ref, irv.at[s, 0], zp)
        ref = part(s, xo, yh, col)
        take_all(ref, crv.at[s, 2])
        out(s, 9, ref, crv.at[s, 6], other)
        out(s, 10, ref, irv.at[s, 0], zm)

    def ego(s):
        ref = part(s, xm, 1 - yh, col)
        take_all(ref, crv.at[s, 4])
        out(s, 11, ref, irv.at[s, 1], zp)
        ref = part(s, xp, 1 - yh, col)
        take_all(ref, crv.at[s, 5])
        out(s, 12, ref, irv.at[s, 1], zm)
        ref = part(s, xo, 1 - yh, col)
        take_all(ref, crv.at[s, 6])
        out(s, 13, ref, irv.at[s, 1], same)

    def hgo(s):
        _, W, cols = stage(s)
        take_all(W.at[pl.ds(0, 3), yh, c, 1 - col, :, cols], irv.at[s, 0])
        out(s, 14, W.at[:, yh, c, :, :, cols], srv.at[s, 0], sibling)

    def igo(s):
        _, W, cols = stage(s)
        take_all(W.at[:, 1 - yh, c, 1 - col, :, cols], irv.at[s, 1])
        out(s, 15, W.at[:, 1 - yh, c, :, :, cols], srv.at[s, 1], sibling)

    def whole(s):
        _, W, cols = stage(s)
        take_all(W.at[:, yh, 1 - c, :, :, cols], srv.at[s, 0])
        take_all(W.at[:, 1 - yh, 1 - c, :, :, cols], srv.at[s, 1])

    def compute(s):
        if s < S1:

            @pl.loop(0, 8 // S1)
            def _(n):
                at = pl.ds(pl.multiple_of(s * (2048 // S1) + n * 256, 256), 256)
                w = W1[:, :, :, :, :, at].reshape(1024, 256)
                v = dot(tok[...], w) + b_in[:, at]
                g = 0.5 * v * (1.0 + jnp.tanh(0.7978845608 * (v + 0.044715 * (v * v * v))))
                hid[:, at] = g.astype(BF16)
        else:

            @pl.loop(0, 4 // S2)
            def _(n):
                at = pl.ds(pl.multiple_of((s - S1) * (1024 // S2) + n * 256, 256), 256)
                w = W2[:, :, :, :, :, at].reshape(2048, 256)
                summed[:, at] = tok[:, at].astype(F32) + dot(hid[...], w) + b_out[:, at]

    ago(0)
    ago(1)
    keep1 = pltpu.make_async_copy(win.at[c], W1.at[x, yh, c], loc.at[0])
    keep2 = pltpu.make_async_copy(wout.at[c], W2.at[x, yh, c], loc.at[1])
    keep1.start()
    keep2.start()

    @pl.loop(0, NZ - 1)
    def _(n):
        to = z_peer(z_at(n))
        send(qf16.at[z], qf16.at[z], psend.at[0], zq.at[0], to)
        send(idsb.at[z], idsb.at[z], psend.at[1], zi.at[0], to)

    leaving.append((qf16.at[pl.ds(0, NZ - 1)], psend.at[0]))
    leaving.append((idsb.at[pl.ds(0, NZ - 1)], psend.at[1]))

    keep1.wait()
    keep2.wait()
    for copy in fetched[3:]:
        copy.wait()

    def prep_column():
        take_all(qf16.at[pl.ds(0, NZ - 1)], zq.at[0])
        flat = qf16[...].reshape(NZ * 16, 256)
        for j in range(4):
            sel = pick(iota((64, 256), 1) == 4 * iota((64, 256), 0) + j)
            rows = dot(sel, flat).astype(BF16)
            qfs[2 * j] = rows[:, :128]
            qfs[2 * j + 1] = rows[:, 128:]
        qfr[f] = qfs[f]

    def prep_query():
        flat = qf16[...].reshape(NZ * 16, 256)
        total_q = jnp.zeros((128, 1024), F32)
        m = iota((128, 256), 0)
        for j in range(4):
            sel = pick((iota((128, 256), 1) == (m // 8) * 16 + (m % 8) * 4 + j) & (m % 8 < 4))
            rows = dot(sel, flat).astype(BF16)
            total_q = total_q + dot(rows, head[j * 256 : (j + 1) * 256, :])
        query[...] = total_q.astype(BF16)
        queryf[...] = query[...].astype(F32)


    def prep_count():
        take_all(idsb.at[pl.ds(0, NZ - 1)], zi.at[0])
        idst[...] = jnp.transpose(idsb[...].reshape(128, 128).astype(F32))
        pi = iota((128, 1), 0)
        pid = (((pi // 64) * 32 + z * 2 + (pi // 32) % 2) * NF + (pi // 4) % NF) * 4 + pi % 4
        pid = pid.astype(F32)
        cT[...] = lax.fori_loop(
            0, 64,
            lambda t, a: a + (idst[pl.ds(t, 1), :] == pid).astype(F32),
            jnp.zeros((128, 128), F32),
        )


    extra = {1: prep_column, 3: prep_query, 4: prep_count}
    NS = S1 + S2
    for tick in range(1, NS + 4):
        if tick <= NS:
            bgo(tick - 1)
            if tick + 1 < NS:
                ago(tick + 1)
        if 0 <= tick - 2 < NS:
            ego(tick - 2)
            hgo(tick - 2)
        if 0 <= tick - 3 < NS:
            igo(tick - 3)
        if tick in extra:
            extra[tick]()
        if 0 <= tick - 4 < NS:
            whole(tick - 4)
            compute(tick - 4)

    rows = []
    for i in range(4):
        v = summed[i * SEQ : (i + 1) * SEQ, :]
        center = v - jnp.mean(v, axis=-1, keepdims=True)
        spread_ = jnp.mean(center * center, axis=-1, keepdims=True)
        normed = center * lax.rsqrt(spread_ + eps)
        rows.append(jnp.sum(normed, axis=0, keepdims=True) * (1.0 / SEQ) * gain[...] + bias[...])
    pooled = jnp.concatenate(rows, axis=0)
    emb[...] = pooled.astype(BF16)
    r16[d] = spread(pooled)

    @pl.loop(1, NPLANE)
    def _(i):
        send(r16.at[d], r16.at[d], psend.at[4], rp.at[0], plane_peer(i))

    leaving.append((r16.at[pl.ds(0, NPLANE - 1)], psend.at[4]))

    lane = iota((1, 128), 1)
    mine = (lane // 8 == z) & (lane % 8 < 4)
    s_col = score_scale * jnp.sum(
        queryf[pl.ds(pl.multiple_of(z * 8, 8), 8), :] * posf[...], axis=-1, keepdims=True
    )
    s_pos = jnp.sum(
        jnp.where(iota((8, 128), 1) == z * 8 + iota((8, 128), 0), s_col, 0.0), axis=0, keepdims=True
    )

    take_all(r16.at[pl.ds(0, NPLANE - 1)], rp.at[0])
    flat_r = r16[...].reshape(NPLANE * 16, 256)
    s = jnp.zeros((128, 128), F32)
    for j in range(4):
        sel = pick(iota((128, 512), 1) == 4 * iota((128, 512), 0) + j)
        rows = dot(sel, flat_r).astype(BF16)
        rk[j] = rows
        s = s + dot(rows, query[:, j * 256 : (j + 1) * 256], (1, 1))
    s = s * score_scale
    count = cT[...]
    listed = count > 0.0
    high = jnp.max(jnp.where(listed, s, LOW), axis=0, keepdims=True)
    part = jnp.sum(
        jnp.where(listed, count * jnp.exp(jnp.where(listed, s - high, 0.0)), 0.0), axis=0, keepdims=True
    )
    high2 = jnp.where(mine, jnp.maximum(high, s_pos), high)
    part2 = part * jnp.exp(high - high2) + jnp.where(mine, jnp.exp(s_pos - high2), 0.0)
    r8 = iota((8, 128), 0)
    stb[z] = jnp.where(r8 == 0, high2, jnp.where(r8 == 1, part2, 0.0))

    @pl.loop(0, NZ - 1)
    def _(n):
        send(stb.at[z], stb.at[z], psend.at[5], zs.at[0], z_peer(z_at(n)))

    leaving.append((stb.at[pl.ds(0, NZ - 1)], psend.at[5]))

    @pl.loop(1, NF)
    def _(i):
        to = f_at(i)
        send(qfs.at[to], qfr.at[f], psend.at[2], fq.at[0], (dp, to))

    leaving.append((qfr.at[pl.ds(0, NF - 1)], psend.at[2]))

    @pl.loop(1, NPLANE)
    def _(i):
        send(pos16.at[d], pos16.at[d], psend.at[3], pp.at[0], plane_peer(i))

    leaving.append((pos16.at[pl.ds(0, NPLANE - 1)], psend.at[3]))

    take_all(stb.at[pl.ds(0, NZ - 1)], zs.at[0])
    stats = stb[...]
    highs, parts = stats[:, 0, :], stats[:, 1, :]
    top = jnp.max(highs, axis=0, keepdims=True)
    total = top + jnp.log(jnp.sum(parts * jnp.exp(highs - top), axis=0, keepdims=True))
    loss[...] = jnp.where(r8 == 0, jnp.where(mine, total - s_pos, 0.0), 0.0)
    coeff = jnp.where(mine, jnp.exp(jnp.where(mine, s_pos - total, 0.0)) - 1.0, 0.0)
    w = jnp.exp(jnp.where(listed, s - total, 0.0)).astype(BF16).astype(F32)
    w = jnp.where(listed, count * w, 0.0).astype(BF16)
    j64 = iota((64, 128), 0)
    wr[f, 0:64, :] = dot(pick(iota((64, 128), 1) == (j64 // 4) * 8 + j64 % 4), w, (1, 1)).astype(BF16)
    c0 = coeff.astype(BF16).astype(F32)
    c1 = (coeff - c0).astype(BF16).astype(F32)
    c2 = coeff - c0 - c1
    r16i = iota((16, 128), 0)
    wr[f, 64:80, :] = jnp.where(
        r16i == 0, c0, jnp.where(r16i == 1, c1, jnp.where(r16i == 2, c2, 0.0))
    ).astype(BF16)

    @pl.loop(1, NF)
    def _(i):
        send(wr.at[f], wr.at[f], psend.at[6], fw.at[0], (dp, f_at(i)))

    leaving.append((wr.at[pl.ds(0, NF - 1)], psend.at[6]))

    take_all(pos16.at[pl.ds(0, NPLANE - 1)], pp.at[0])
    flat_p = pos16[...].reshape(NPLANE * 16, 256)
    for j in range(4):
        sel = pick(iota((128, 512), 1) == 4 * iota((128, 512), 0) + j)
        pk[j] = dot(sel, flat_p).astype(BF16)
    take_all(qfr.at[pl.ds(0, NF - 1)], fq.at[0])
    slices = qfr[...].reshape(NF * 64, 128)
    g32 = iota((32, 512), 0)
    group_q = dot(pick(iota((32, 512), 1) == (g32 // 4) * 64 + z * 4 + g32 % 4), slices)

    take_all(wr.at[pl.ds(0, NF - 1)], fw.at[0])
    g_part = dot(slices, wr[:, 0:64, :].reshape(NF * 64, 128), (0, 0)).astype(BF16)
    e32, l32 = iota((32, 128), 0), iota((32, 128), 1)
    expand = pick((l32 // 16 == e32 // 4) & (l32 % 16 < 3))
    co = dot(expand, wr[:, 64:80, :].reshape(128, 128))
    co = jnp.sum(jnp.where(l32 == z * 8 + e32 % 4, co, 0.0), axis=1, keepdims=True)
    g_pos = (group_q * co).astype(BF16)
    shift = pick(l32 == k * 32 + e32)
    g_pos = dot(g_pos, shift, (0, 0)).astype(BF16)
    for e in range(4):
        gs[e, 0:32, :] = g_part[e * 32 : e * 32 + 32, :]
        gs[e, 32:64, :] = g_pos[e * 32 : e * 32 + 32, :]
    gr[k] = gs[k]

    @pl.loop(1, 4)
    def _(i):
        to = (k + i) % 4
        send(gs.at[to], gr.at[k], psend.at[7], gx.at[0], quarter_peer(i))

    leaving.append((gr.at[pl.ds(0, 3)], psend.at[7]))

    take_all(gr.at[pl.ds(0, 3)], gx.at[0])
    g_all = jnp.sum(gr[...].astype(F32), axis=0).astype(BF16)
    for e in range(4):
        term = score_scale * (dot(g_all[0:32, :], rk[e]) + dot(g_all[32:64, :], pk[e]))
        term = term.astype(BF16)
        for t in range(4):
            rss[e * 2 + t % 2 + 8 * (t // 2)] = term[(t // 2) * 16 : (t // 2) * 16 + 16, (t % 2) * 128 : (t % 2) * 128 + 128]
    rsr[z] = rss[z]

    @pl.loop(0, NZ - 1)
    def _(n):
        to = z_at(n)
        send(rss.at[to], rsr.at[z], psend.at[8], zr.at[0], z_peer(to))

    leaving.append((rsr.at[pl.ds(0, NZ - 1)], psend.at[8]))

    take_all(rsr.at[pl.ds(0, NZ - 1)], zr.at[0])
    agr[k, z] = jnp.sum(rsr[...].astype(F32), axis=0).astype(BF16)

    @pl.loop(0, NZ - 1)
    def _(n):
        send(agr.at[k, z], agr.at[k, z], psend.at[9], za.at[0], z_peer(z_at(n)))

    leaving.append((agr.at[0, pl.ds(0, NZ - 1)], psend.at[9]))

    take_all(agr.at[k, pl.ds(0, NZ - 1)], za.at[0])

    @pl.loop(1, 4)
    def _(i):
        send(agr.at[k], agr.at[k], psend.at[10], ga.at[0], quarter_peer(i))

    leaving.append((agr.at[pl.ds(0, 3)], psend.at[10]))

    take_all(agr.at[pl.ds(0, 3)], ga.at[0])
    for e in range(4):
        for t in range(NZ):
            row, at = e * 32 + (t // 8) * 16, (t % 8) * 128
            hg[row : row + 16, at : at + 128] = agr[e, t].astype(F32)

    for copy in sent:
        copy.wait_send()
    for ref, sem in leaving:
        take_all(ref, sem)


def body(
    tokens, w_in, b_in, w_out, b_out, ln_gain, ln_bias, head, query_feats, positive_rows, neg_ids
):
    vmem = pl.BlockSpec(memory_space=pltpu.VMEM)
    V, S = pltpu.VMEM, pltpu.SemaphoreType.DMA
    embedded, loss, head_grad = pl.pallas_call(
        kernel,
        out_shape=(
            jax.ShapeDtypeStruct((4, 1024), BF16),
            jax.ShapeDtypeStruct((8, 128), F32),
            jax.ShapeDtypeStruct((128, 1024), F32),
        ),
        in_specs=[pl.BlockSpec(memory_space=pl.ANY)] * 11,
        out_specs=(vmem,) * 3,
        scratch_shapes=[
            V((512, 1024), BF16),
            V((1, 2048), F32),
            V((1, 1024), F32),
            V((1, 1024), F32),
            V((1, 1024), F32),
            V((1024, 1024), BF16),
            V((4, 1024), BF16),
            V((4, 1024), BF16),
            V((4, 64), jnp.int32),
            S((9,)),
            V((4, 2, 2, 2, 32, 2048), BF16),
            V((4, 2, 2, 2, 64, 1024), BF16),
            V((512, 2048), BF16),
            V((512, 1024), F32),
            V((16, 256), F32),
            V((NZ, 16, 256), BF16),
            V((NZ, 8, 128), jnp.int32),
            V((NPLANE, 16, 256), BF16),
            V((NPLANE, 16, 256), BF16),
            V((NF, 64, 128), BF16),
            V((NF, 64, 128), BF16),
            V((128, 1024), BF16),
            V((128, 1024), F32),
            V((8, 1024), F32),
            V((128, 128), F32),
            V((128, 128), F32),
            V((4, 128, 256), BF16),
            V((4, 128, 256), BF16),
            V((NZ, 8, 128), F32),
            V((NF, 80, 128), BF16),
            V((4, 64, 128), BF16),
            V((4, 64, 128), BF16),
            V((NZ, 16, 128), BF16),
            V((NZ, 16, 128), BF16),
            V((4, NZ, 16, 128), BF16),
        ]
        + [S((S1 + S2, 7)), S((S1 + S2, 2)), S((S1 + S2, 2)), S((S1 + S2, 16)), S((2,))]
        + [S((1,))] * 11
        + [S((11,))],
        compiler_params=pltpu.CompilerParams(
            collective_id=0, has_side_effects=True, vmem_limit_bytes=60 << 20
        ),
    )(
        tokens,
        w_in.reshape(2, 2, 32, 2048),
        b_in.reshape(1, -1),
        w_out.reshape(2, 2, 64, 1024),
        b_out.reshape(1, -1),
        ln_gain.reshape(1, -1),
        ln_bias.reshape(1, -1),
        head,
        query_feats,
        positive_rows,
        neg_ids,
    )
    z = (lax.axis_index("dp") // 2) % NZ
    return embedded, lax.dynamic_slice_in_dim(loss[0], z * 8, 4), head_grad


def solution(mesh):
    in_specs = (
        P(("dp", "fsdp"), None),
        P("fsdp", None),
        P(),
        P("fsdp", None),
        P(),
        P(),
        P(),
        P(),
        P(("dp", "fsdp"), None),
        P(("dp", "fsdp"), None),
        P(("dp", "fsdp"), None),
    )
    out_specs = (P(("dp", "fsdp"), None), P(("dp", "fsdp")), P("fsdp", None))
    return jax.shard_map(body, mesh=mesh, in_specs=in_specs, out_specs=out_specs, check_vma=False)
```

```python
import jax
import jax.numpy as jnp
from jax import lax
from jax.experimental import pallas as pl
from jax.experimental.pallas import tpu as pltpu
from jax.sharding import PartitionSpec as P

SEQ = 128
NX, NZ, NF, NPLANE = 4, 16, 8, 32
WIDTHS1, WIDTHS2 = (1024, 1024), (512, 512)
NS = len(WIDTHS1) + len(WIDTHS2)
score_scale = 0.5
eps = 1e-05
LOW = -3.0e38
MESH = pl.DeviceIdType.MESH
div, rem = lax.div, lax.rem
F32, BF16 = jnp.float32, jnp.bfloat16


def iota(shape, dim):
    return lax.broadcasted_iota(jnp.int32, shape, dim)


def dot(a, b, dims=(1, 0)):
    return lax.dot_general(
        a, b, (((dims[0],), (dims[1],)), ((), ())), preferred_element_type=F32
    )


def hi(a, n):
    return lax.shift_right_logical(a, jnp.full(a.shape, n.bit_length() - 1, jnp.int32))


def lo(a, n):
    return a & (n - 1)


def pick(mask):
    return mask.astype(F32).astype(BF16)


def take_all(ref, sem):
    pltpu.make_async_copy(ref, ref, sem).wait()


def kernel(
    tok_h, win, b_in_h, wout, b_out_h, gain_h, bias_h, head_h, feats_h, pos_h, ids_h,
    emb, loss, grads,
    tok, b_in, b_out, gain, bias, head, feats, pos, ids, inp,
    W1, W2, hid, summed, stg, qf16, idsb, pos16, r16, qfs, qfr, query, queryf, posf, idst, cT, rk,
    pk, selr, stb, wr, gs, gr, rss, rsr, agr,
    crv, irv, srv, ssend, loc,
    zq, zi, pp, fq, rp, zs, fw, gx, zr, za, ga, psend,
):
    dp, f = lax.axis_index("dp"), lax.axis_index("fsdp")
    yl, z, c = div(dp, 32), rem(div(dp, 2), NZ), rem(dp, 2)
    x, yh = div(f, 2), rem(f, 2)
    k = yl * 2 + c
    d = k * NF + f

    y = 2 * yh + yl
    xs = [x] + [rem(x + i, NX) for i in range(1, NX)]
    zz = [z] + [rem(z + i, NZ) for i in range(1, NZ)]
    yhs, yls = [yh], [yl]
    for i in range(1, 4):
        v = rem(y + i, 4)
        yhs.append(div(v, 2))
        yls.append(rem(v, 2))
    cs = [c, 1 - c]
    dps = [[v * 32 + z * 2 + w for w in cs] for v in yls]
    fs = [[v * 2 + w for w in yhs] for v in xs]
    plane = [
        (dps[j][w], fs[i][j]) for i in (2, 3, 1, 0) for j in (2, 3, 1, 0) for w in (1, 0) if i or j or w
    ]
    column = [(zz[i], (yl * 32 + zz[i] * 2 + c, f)) for i in (8, 9, 7, 10, 6, 11, 5, 12, 4, 13, 3, 14, 2, 15, 1)]
    row = [xs[i] * 2 + v for i in (2, 3, 1, 0) for v in (1 - yh, yh)][:-1]
    quarter = [
        (v * 2 + w, (v * 32 + z * 2 + w, f)) for v, w in ((1 - yl, 1 - c), (1 - yl, c), (yl, 1 - c))
    ]
    right, left, far = (dp, fs[1][0]), (dp, fs[3][0]), (dp, fs[2][0])
    other, same = ((1 - yl) * 32 + z * 2 + c, x * 2 + 1 - yh), ((1 - yl) * 32 + z * 2 + c, f)
    sibling = (dps[0][1], f)
    zp, zm = column[-1][1], column[-2][1]

    def send(src, dst, ss, rs, to):
        copy = pltpu.make_async_remote_copy(
            src_ref=src, dst_ref=dst, send_sem=ss, recv_sem=rs, device_id=to, device_id_type=MESH
        )
        copy.start()
        return copy

    barrier = pltpu.get_barrier_semaphore()

    for _, to in column:
        pl.semaphore_signal(barrier, inc=1, device_id=to, device_id_type=MESH)

    for to in plane:
        pl.semaphore_signal(barrier, inc=1, device_id=to, device_id_type=MESH)

    fetched = [
        pltpu.make_async_copy(a, b, inp.at[i])
        for i, (a, b) in enumerate(
            [(feats_h, feats), (pos_h, pos), (ids_h, ids), (tok_h, tok), (head_h, head),
             (b_in_h, b_in), (b_out_h, b_out), (gain_h, gain), (bias_h, bias)]
        )
    ]
    for copy in fetched:
        copy.start()

    def spread(rows):
        for i in range(4):
            for j in range(4):
                stg[pl.ds(i * 4 + j, 1), :] = rows[i : i + 1, j * 256 : (j + 1) * 256]
        return stg[...].astype(BF16)

    for copy in fetched[:3]:
        copy.wait()
    qf16[z] = spread(feats[...].astype(F32))
    pos16[d] = spread(pos[...].astype(F32))
    posf[...] = jnp.zeros_like(posf)
    posf[0:4, :] = pos[...].astype(F32)
    idsb[z] = jnp.full((8, 128), -1, jnp.int32)
    idsb[z, 0:4, 0:64] = ids[...]

    pl.semaphore_wait(barrier, NPLANE - 1 + NZ - 1)

    col = rem(z + yl + yh, 2)
    xm, xp, xo = xs[3], xs[1], xs[2]

    def stage(s):
        if s < len(WIDTHS1):
            return win, W1, pl.ds(sum(WIDTHS1[:s]), WIDTHS1[s])
        s -= len(WIDTHS1)
        return wout, W2, pl.ds(sum(WIDTHS2[:s]), WIDTHS2[s])

    sent, leaving = [], []

    def out(s, n, ref, rs, to, src=None):
        sent.append(send(ref if src is None else src, ref, ssend.at[s, n], rs, to))

    def part(s, xx, hh, half):
        _, W, cols = stage(s)
        return W.at[xx, hh, c, half, :, cols]

    def ago(s):
        shard, _, cols = stage(s)
        ref, src = part(s, x, yh, col), shard.at[c, col, :, cols]
        out(s, 0, ref, crv.at[s, 0], right, src)
        out(s, 1, ref, crv.at[s, 1], left, src)
        out(s, 2, ref, crv.at[s, 3], other, src)
        out(s, 3, ref, crv.at[s, 2], far, src)

    def bgo(s):
        ref = part(s, x, 1 - yh, col)
        take_all(ref, crv.at[s, 3])
        out(s, 4, ref, crv.at[s, 4], right)
        out(s, 5, ref, crv.at[s, 5], left)
        out(s, 6, ref, irv.at[s, 1], same)
        ref = part(s, xm, yh, col)
        take_all(ref, crv.at[s, 0])
        out(s, 7, ref, irv.at[s, 0], same)
        ref = part(s, xp, yh, col)
        take_all(ref, crv.at[s, 1])
        out(s, 8, ref, irv.at[s, 0], zp)
        ref = part(s, xo, yh, col)
        take_all(ref, crv.at[s, 2])
        out(s, 9, ref, crv.at[s, 6], other)
        out(s, 10, ref, irv.at[s, 0], zm)

    def ego(s):
        ref = part(s, xm, 1 - yh, col)
        take_all(ref, crv.at[s, 4])
        out(s, 11, ref, irv.at[s, 1], zp)
        ref = part(s, xp, 1 - yh, col)
        take_all(ref, crv.at[s, 5])
        out(s, 12, ref, irv.at[s, 1], zm)
        ref = part(s, xo, 1 - yh, col)
        take_all(ref, crv.at[s, 6])
        out(s, 13, ref, irv.at[s, 1], same)

    def hgo(s):
        _, W, cols = stage(s)
        take_all(W.at[pl.ds(0, 3), yh, c, 1 - col, :, cols], irv.at[s, 0])
        out(s, 14, W.at[:, yh, c, :, :, cols], srv.at[s, 0], sibling)

    def igo(s):
        _, W, cols = stage(s)
        take_all(W.at[:, 1 - yh, c, 1 - col, :, cols], irv.at[s, 1])
        out(s, 15, W.at[:, 1 - yh, c, :, :, cols], srv.at[s, 1], sibling)

    def whole(s):
        _, W, cols = stage(s)
        take_all(W.at[:, yh, 1 - c, :, :, cols], srv.at[s, 0])
        take_all(W.at[:, 1 - yh, 1 - c, :, :, cols], srv.at[s, 1])

    def compute(s):
        _, W, cols = stage(s)

        @pl.loop(0, cols.size // 256)
        def _(n):
            at = pl.ds(pl.multiple_of(cols.start + n * 256, 256), 256)
            w = W[:, :, :, :, :, at].reshape(-1, 256)
            if W is W1:
                v = dot(tok[...], w) + b_in[:, at]
                g = 0.5 * v * (1.0 + jnp.tanh(0.7978845608 * (v + 0.044715 * (v * v * v))))
                hid[:, at] = g.astype(BF16)
            else:
                summed[:, at] = tok[:, at].astype(F32) + dot(hid[...], w) + b_out[:, at]

    ago(0)
    ago(1)
    keep1 = pltpu.make_async_copy(win.at[c], W1.at[x, yh, c], loc.at[0])
    keep2 = pltpu.make_async_copy(wout.at[c], W2.at[x, yh, c], loc.at[1])
    keep1.start()
    keep2.start()

    for _, to in column:
        send(qf16.at[z], qf16.at[z], psend.at[0], zq.at[0], to)
        send(idsb.at[z], idsb.at[z], psend.at[1], zi.at[0], to)

    leaving.append((qf16.at[pl.ds(0, NZ - 1)], psend.at[0]))
    leaving.append((idsb.at[pl.ds(0, NZ - 1)], psend.at[1]))

    for j in range(4):
        selr[j] = pick(iota((128, 512), 1) == 4 * iota((128, 1), 0) + j)

    keep1.wait()
    keep2.wait()
    for copy in fetched[3:]:
        copy.wait()

    def prep_column():
        flat = qf16[...].reshape(NZ * 16, 256)
        for j in range(4):
            sel = pick(iota((64, 256), 1) == 4 * iota((64, 1), 0) + j)
            rows = dot(sel, flat).astype(BF16)
            qfs[2 * j] = rows[:, :128]
            qfs[2 * j + 1] = rows[:, 128:]
        qfr[f] = qfs[f]

    def prep_query():
        take_all(qf16.at[pl.ds(0, NZ - 1)], zq.at[0])
        flat = qf16[...].reshape(NZ * 16, 256)
        total_q = jnp.zeros((128, 1024), F32)
        m = iota((128, 1), 0)
        at = jnp.where(lo(m, 8) < 4, hi(m, 8) * 16 + lo(m, 8) * 4, -8)
        for j in range(4):
            sel = pick(iota((128, 256), 1) == at + j)
            rows = dot(sel, flat).astype(BF16)
            total_q = total_q + dot(rows, head[j * 256 : (j + 1) * 256, :])
        query[...] = total_q.astype(BF16)
        queryf[...] = query[...].astype(F32)


    def prep_count():
        take_all(idsb.at[pl.ds(0, NZ - 1)], zi.at[0])
        idst[...] = jnp.transpose(idsb[...].reshape(128, 128).astype(F32))
        pi = iota((128, 1), 0)
        pid = ((hi(pi, 64) * 32 + z * 2 + lo(hi(pi, 32), 2)) * NF + lo(hi(pi, 4), NF)) * 4 + lo(pi, 4)
        pid = pid.astype(F32)
        cT[...] = lax.fori_loop(
            0, 64,
            lambda t, a: a + (idst[pl.ds(t, 1), :] == pid).astype(F32),
            jnp.zeros((128, 128), F32),
        )


    extra = {3: prep_query}
    for tick in range(1, NS + 4):
        if tick <= NS:
            bgo(tick - 1)
            if tick + 1 < NS:
                ago(tick + 1)
        if 0 <= tick - 2 < NS:
            ego(tick - 2)
            hgo(tick - 2)
        if 0 <= tick - 3 < NS:
            igo(tick - 3)
        if tick in extra:
            extra[tick]()
        if 0 <= tick - 4 < NS:
            whole(tick - 4)
            compute(tick - 4)

    rows = []
    for i in range(4):
        v = summed[i * SEQ : (i + 1) * SEQ, :]
        center = v - jnp.mean(v, axis=-1, keepdims=True)
        spread_ = jnp.mean(center * center, axis=-1, keepdims=True)
        normed = center * lax.rsqrt(spread_ + eps)
        rows.append(jnp.sum(normed, axis=0, keepdims=True) * (1.0 / SEQ) * gain[...] + bias[...])
    pooled = jnp.concatenate(rows, axis=0)
    emb[...] = pooled.astype(BF16)
    r16[d] = spread(pooled)

    for to in plane:
        send(r16.at[d], r16.at[d], psend.at[4], rp.at[0], to)

    leaving.append((r16.at[pl.ds(0, NPLANE - 1)], psend.at[4]))

    prep_count()
    prep_column()
    lane = iota((1, 128), 1)
    mine = (hi(lane, 8) == z) & (lo(lane, 8) < 4)
    s_col = score_scale * jnp.sum(
        queryf[pl.ds(pl.multiple_of(z * 8, 8), 8), :] * posf[...], axis=-1, keepdims=True
    )
    s_pos = jnp.sum(
        jnp.where(iota((8, 128), 1) == z * 8 + iota((8, 128), 0), s_col, 0.0), axis=0, keepdims=True
    )

    take_all(r16.at[pl.ds(0, NPLANE - 1)], rp.at[0])
    flat_r = r16[...].reshape(NPLANE * 16, 256)
    s = jnp.zeros((128, 128), F32)
    for j in range(4):
        rows = dot(selr[j], flat_r).astype(BF16)
        rk[j] = rows
        s = s + dot(rows, query[:, j * 256 : (j + 1) * 256], (1, 1))
    s = s * score_scale
    count = cT[...]
    listed = count > 0.0
    high = jnp.max(jnp.where(listed, s, LOW), axis=0, keepdims=True)
    part = jnp.sum(
        jnp.where(listed, count * jnp.exp(jnp.where(listed, s - high, 0.0)), 0.0), axis=0, keepdims=True
    )
    high2 = jnp.where(mine, jnp.maximum(high, s_pos), high)
    part2 = part * jnp.exp(high - high2) + jnp.where(mine, jnp.exp(s_pos - high2), 0.0)
    r8 = iota((8, 128), 0)
    stb[z] = jnp.where(r8 == 0, high2, jnp.where(r8 == 1, part2, 0.0))

    for _, to in column:
        send(stb.at[z], stb.at[z], psend.at[5], zs.at[0], to)

    leaving.append((stb.at[pl.ds(0, NZ - 1)], psend.at[5]))

    for to in row:
        send(qfs.at[to], qfr.at[f], psend.at[2], fq.at[0], (dp, to))

    leaving.append((qfr.at[pl.ds(0, NF - 1)], psend.at[2]))

    for to in plane:
        send(pos16.at[d], pos16.at[d], psend.at[3], pp.at[0], to)

    leaving.append((pos16.at[pl.ds(0, NPLANE - 1)], psend.at[3]))

    j64 = iota((64, 1), 0)
    squeeze = pick(iota((64, 128), 1) == hi(j64, 4) * 8 + lo(j64, 4))

    take_all(stb.at[pl.ds(0, NZ - 1)], zs.at[0])
    stats = stb[...]
    highs, parts = stats[:, 0, :], stats[:, 1, :]
    top = jnp.max(highs, axis=0, keepdims=True)
    total = top + jnp.log(jnp.sum(parts * jnp.exp(highs - top), axis=0, keepdims=True))
    loss[...] = jnp.where(r8 == 0, jnp.where(mine, total - s_pos, 0.0), 0.0)
    coeff = jnp.where(mine, jnp.exp(jnp.where(mine, s_pos - total, 0.0)) - 1.0, 0.0)
    w = jnp.exp(jnp.where(listed, s - total, 0.0)).astype(BF16).astype(F32)
    w = jnp.where(listed, count * w, 0.0).astype(BF16)
    wr[f, 0:64, :] = dot(squeeze, w, (1, 1)).astype(BF16)
    c0 = coeff.astype(BF16).astype(F32)
    c1 = (coeff - c0).astype(BF16).astype(F32)
    c2 = coeff - c0 - c1
    r16i = iota((16, 128), 0)
    wr[f, 64:80, :] = jnp.where(
        r16i == 0, c0, jnp.where(r16i == 1, c1, jnp.where(r16i == 2, c2, 0.0))
    ).astype(BF16)

    for to in row:
        send(wr.at[f], wr.at[f], psend.at[6], fw.at[0], (dp, to))

    leaving.append((wr.at[pl.ds(0, NF - 1)], psend.at[6]))

    take_all(pos16.at[pl.ds(0, NPLANE - 1)], pp.at[0])
    flat_p = pos16[...].reshape(NPLANE * 16, 256)
    for j in range(4):
        pk[j] = dot(selr[j], flat_p).astype(BF16)
    take_all(qfr.at[pl.ds(0, NF - 1)], fq.at[0])
    slices = qfr[...].reshape(NF * 64, 128)
    e32, l32 = iota((32, 1), 0), iota((32, 128), 1)
    group_q = dot(pick(iota((32, 512), 1) == hi(e32, 4) * 64 + z * 4 + lo(e32, 4)), slices)
    expand = pick((hi(l32, 16) == hi(e32, 4)) & (lo(l32, 16) < 3))
    own_lane = l32 == z * 8 + lo(e32, 4)
    shift = pick(l32 == k * 32 + e32)

    take_all(wr.at[pl.ds(0, NF - 1)], fw.at[0])
    g_part = dot(slices, wr[:, 0:64, :].reshape(NF * 64, 128), (0, 0)).astype(BF16)
    co = dot(expand, wr[:, 64:80, :].reshape(128, 128))
    co = jnp.sum(jnp.where(own_lane, co, 0.0), axis=1, keepdims=True)
    g_pos = (group_q * co).astype(BF16)
    g_pos = dot(g_pos, shift, (0, 0)).astype(BF16)
    for e in range(4):
        gs[e, 0:32, :] = g_part[e * 32 : e * 32 + 32, :]
        gs[e, 32:64, :] = g_pos[e * 32 : e * 32 + 32, :]
    gr[k] = gs[k]

    for n, to in quarter:
        send(gs.at[n], gr.at[k], psend.at[7], gx.at[0], to)

    leaving.append((gr.at[pl.ds(0, 3)], psend.at[7]))

    take_all(gr.at[pl.ds(0, 3)], gx.at[0])
    g_all = jnp.sum(gr[...].astype(F32), axis=0).astype(BF16)
    for e in range(4):
        term = score_scale * (dot(g_all[0:32, :], rk[e]) + dot(g_all[32:64, :], pk[e]))
        term = term.astype(BF16)
        for t in range(4):
            rss[e * 2 + t % 2 + 8 * (t // 2)] = term[(t // 2) * 16 : (t // 2) * 16 + 16, (t % 2) * 128 : (t % 2) * 128 + 128]
    rsr[z] = rss[z]

    for n, to in column:
        send(rss.at[n], rsr.at[z], psend.at[8], zr.at[0], to)

    leaving.append((rsr.at[pl.ds(0, NZ - 1)], psend.at[8]))

    take_all(rsr.at[pl.ds(0, NZ - 1)], zr.at[0])
    agr[k, z] = jnp.sum(rsr[...].astype(F32), axis=0).astype(BF16)

    for _, to in column:
        send(agr.at[k, z], agr.at[k, z], psend.at[9], za.at[0], to)

    leaving.append((agr.at[0, pl.ds(0, NZ - 1)], psend.at[9]))

    take_all(agr.at[k, pl.ds(0, NZ - 1)], za.at[0])

    for _, to in quarter:
        send(agr.at[k], agr.at[k], psend.at[10], ga.at[0], to)

    leaving.append((agr.at[pl.ds(0, 3)], psend.at[10]))

    take_all(agr.at[pl.ds(0, 3)], ga.at[0])
    grads[...] = agr[...]

    for copy in sent:
        copy.wait_send()
    for ref, sem in leaving:
        take_all(ref, sem)


def finish(emb_in, loss_in, parts, emb, loss, hg):
    z = rem(div(lax.axis_index("dp"), 2), NZ)
    emb[...] = emb_in[...]
    row, lane = loss_in[0:1, :], iota((1, 128), 1)
    for i in range(4):
        loss[i] = jnp.sum(jnp.where(lane == z * 8 + i, row, 0.0))
    for e in range(4):
        for t in range(NZ):
            row, at = e * 32 + (t // 8) * 16, (t % 8) * 128
            hg[row : row + 16, at : at + 128] = parts[e, t].astype(F32)


def body(
    tokens, w_in, b_in, w_out, b_out, ln_gain, ln_bias, head, query_feats, positive_rows, neg_ids
):
    vmem = pl.BlockSpec(memory_space=pltpu.VMEM)
    V, S = pltpu.VMEM, pltpu.SemaphoreType.DMA
    parts = pl.pallas_call(
        kernel,
        out_shape=(
            jax.ShapeDtypeStruct((4, 1024), BF16),
            jax.ShapeDtypeStruct((8, 128), F32),
            jax.ShapeDtypeStruct((4, NZ, 16, 128), BF16),
        ),
        in_specs=[pl.BlockSpec(memory_space=pl.ANY)] * 11,
        out_specs=(vmem,) * 3,
        scratch_shapes=[
            V((512, 1024), BF16),
            V((1, 2048), F32),
            V((1, 1024), F32),
            V((1, 1024), F32),
            V((1, 1024), F32),
            V((1024, 1024), BF16),
            V((4, 1024), BF16),
            V((4, 1024), BF16),
            V((4, 64), jnp.int32),
            S((9,)),
            V((4, 2, 2, 2, 32, 2048), BF16),
            V((4, 2, 2, 2, 64, 1024), BF16),
            V((512, 2048), BF16),
            V((512, 1024), F32),
            V((16, 256), F32),
            V((NZ, 16, 256), BF16),
            V((NZ, 8, 128), jnp.int32),
            V((NPLANE, 16, 256), BF16),
            V((NPLANE, 16, 256), BF16),
            V((NF, 64, 128), BF16),
            V((NF, 64, 128), BF16),
            V((128, 1024), BF16),
            V((128, 1024), F32),
            V((8, 1024), F32),
            V((128, 128), F32),
            V((128, 128), F32),
            V((4, 128, 256), BF16),
            V((4, 128, 256), BF16),
            V((4, 128, 512), BF16),
            V((NZ, 8, 128), F32),
            V((NF, 80, 128), BF16),
            V((4, 64, 128), BF16),
            V((4, 64, 128), BF16),
            V((NZ, 16, 128), BF16),
            V((NZ, 16, 128), BF16),
            V((4, NZ, 16, 128), BF16),
        ]
        + [S((NS, 7)), S((NS, 2)), S((NS, 2)), S((NS, 16)), S((2,))]
        + [S((1,))] * 11
        + [S((11,))],
        compiler_params=pltpu.CompilerParams(
            collective_id=0, has_side_effects=True, vmem_limit_bytes=60 << 20
        ),
    )(
        tokens,
        w_in.reshape(2, 2, 32, 2048),
        b_in.reshape(1, -1),
        w_out.reshape(2, 2, 64, 1024),
        b_out.reshape(1, -1),
        ln_gain.reshape(1, -1),
        ln_bias.reshape(1, -1),
        head,
        query_feats,
        positive_rows,
        neg_ids,
    )
    return pl.pallas_call(
        finish,
        out_shape=(
            jax.ShapeDtypeStruct((4, 1024), BF16),
            jax.ShapeDtypeStruct((4,), F32),
            jax.ShapeDtypeStruct((128, 1024), F32),
        ),
        in_specs=[vmem] * 3,
        out_specs=(vmem, pl.BlockSpec(memory_space=pltpu.SMEM), vmem),
    )(*parts)


def solution(mesh):
    in_specs = (
        P(("dp", "fsdp"), None),
        P("fsdp", None),
        P(),
        P("fsdp", None),
        P(),
        P(),
        P(),
        P(),
        P(("dp", "fsdp"), None),
        P(("dp", "fsdp"), None),
        P(("dp", "fsdp"), None),
    )
    out_specs = (P(("dp", "fsdp"), None), P(("dp", "fsdp")), P("fsdp", None))
    return jax.shard_map(body, mesh=mesh, in_specs=in_specs, out_specs=out_specs, check_vma=False)
```

```python
import jax
import jax.numpy as jnp
from jax import lax
from jax.experimental import pallas as pl
from jax.experimental.pallas import tpu as pltpu
from jax.sharding import PartitionSpec as P

SEQ = 128
NX, NZ, NF, NPLANE = 4, 16, 8, 32
WIDTHS1, WIDTHS2 = (1024, 1024), (512, 512)
NS = len(WIDTHS1) + len(WIDTHS2)
score_scale = 0.5
eps = 1e-05
LOW = -3.0e38
MESH = pl.DeviceIdType.MESH
div, rem = lax.div, lax.rem
F32, BF16 = jnp.float32, jnp.bfloat16


def iota(shape, dim):
    return lax.broadcasted_iota(jnp.int32, shape, dim)


def dot(a, b, dims=(1, 0)):
    return lax.dot_general(
        a, b, (((dims[0],), (dims[1],)), ((), ())), preferred_element_type=F32
    )


def hi(a, n):
    return lax.shift_right_logical(a, jnp.full(a.shape, n.bit_length() - 1, jnp.int32))


def lo(a, n):
    return a & (n - 1)


def pick(mask):
    return mask.astype(F32).astype(BF16)


def take_all(ref, sem):
    pltpu.make_async_copy(ref, ref, sem).wait()


def kernel(
    tok_h, win, b_in_h, wout, b_out_h, gain_h, bias_h, head_h, feats_h, pos_h, ids_h,
    emb, loss, grads,
    tok, b_in, b_out, gain, bias, head, feats, pos, ids, inp,
    W1, W2, hid, summed, stg, qf16, idsb, pos16, r16, qfs, qfr, query, queryf, posf, idst, cT, rk,
    pk, selr, stb, wr, gs, gr, rss, rsr, agr,
    crv, irv, srv, ssend, loc,
    zq, zi, pp, fq, rp, zs, fw, gx, zr, za, ga, psend,
):
    dp, f = lax.axis_index("dp"), lax.axis_index("fsdp")
    yl, z, c = div(dp, 32), rem(div(dp, 2), NZ), rem(dp, 2)
    x, yh = div(f, 2), rem(f, 2)
    k = yl * 2 + c
    d = k * NF + f

    y = 2 * yh + yl
    xs = [x] + [rem(x + i, NX) for i in range(1, NX)]
    zz = [z] + [rem(z + i, NZ) for i in range(1, NZ)]
    yhs, yls = [yh], [yl]
    for i in range(1, 4):
        v = rem(y + i, 4)
        yhs.append(div(v, 2))
        yls.append(rem(v, 2))
    cs = [c, 1 - c]
    dps = [[v * 32 + z * 2 + w for w in cs] for v in yls]
    fs = [[v * 2 + w for w in yhs] for v in xs]
    plane = [
        (dps[j][w], fs[i][j]) for i in (2, 3, 1, 0) for j in (2, 3, 1, 0) for w in (1, 0) if i or j or w
    ]
    column = [(zz[i], (yl * 32 + zz[i] * 2 + c, f)) for i in (8, 9, 7, 10, 6, 11, 5, 12, 4, 13, 3, 14, 2, 15, 1)]
    row = [xs[i] * 2 + v for i in (2, 3, 1, 0) for v in (1 - yh, yh)][:-1]
    quarter = [
        (v * 2 + w, (v * 32 + z * 2 + w, f)) for v, w in ((1 - yl, 1 - c), (1 - yl, c), (yl, 1 - c))
    ]
    right, left, far = (dp, fs[1][0]), (dp, fs[3][0]), (dp, fs[2][0])
    other, same = ((1 - yl) * 32 + z * 2 + c, x * 2 + 1 - yh), ((1 - yl) * 32 + z * 2 + c, f)
    sibling = (dps[0][1], f)
    zp, zm = column[-1][1], column[-2][1]

    def send(src, dst, ss, rs, to):
        copy = pltpu.make_async_remote_copy(
            src_ref=src, dst_ref=dst, send_sem=ss, recv_sem=rs, device_id=to, device_id_type=MESH
        )
        copy.start()
        return copy

    barrier = pltpu.get_barrier_semaphore()

    for _, to in column:
        pl.semaphore_signal(barrier, inc=1, device_id=to, device_id_type=MESH)

    for to in plane:
        pl.semaphore_signal(barrier, inc=1, device_id=to, device_id_type=MESH)

    fetched = [
        pltpu.make_async_copy(a, b, inp.at[i])
        for i, (a, b) in enumerate(
            [(feats_h, feats), (pos_h, pos), (ids_h, ids), (tok_h, tok), (head_h, head),
             (b_in_h, b_in), (b_out_h, b_out), (gain_h, gain), (bias_h, bias)]
        )
    ]
    for copy in fetched:
        copy.start()

    def spread(rows):
        for i in range(4):
            for j in range(4):
                stg[pl.ds(i * 4 + j, 1), :] = rows[i : i + 1, j * 256 : (j + 1) * 256]
        return stg[...].astype(BF16)

    for copy in fetched[:3]:
        copy.wait()
    qf16[z] = spread(feats[...].astype(F32))
    pos16[d] = spread(pos[...].astype(F32))
    posf[...] = jnp.zeros_like(posf)
    posf[0:4, :] = pos[...].astype(F32)
    idsb[z] = jnp.full((8, 128), -1, jnp.int32)
    idsb[z, 0:4, 0:64] = ids[...]

    pl.semaphore_wait(barrier, NPLANE - 1 + NZ - 1)

    col = rem(z + yl + yh, 2)
    xm, xp, xo = xs[3], xs[1], xs[2]

    def stage(s):
        if s < len(WIDTHS1):
            return win, W1, pl.ds(sum(WIDTHS1[:s]), WIDTHS1[s])
        s -= len(WIDTHS1)
        return wout, W2, pl.ds(sum(WIDTHS2[:s]), WIDTHS2[s])

    sent, leaving = [], []

    def out(s, n, ref, rs, to, src=None):
        sent.append(send(ref if src is None else src, ref, ssend.at[s, n], rs, to))

    def part(s, xx, hh, half):
        _, W, cols = stage(s)
        return W.at[xx, hh, c, half, :, cols]

    def ago(s):
        shard, _, cols = stage(s)
        ref, src = part(s, x, yh, col), shard.at[c, col, :, cols]
        out(s, 0, ref, crv.at[s, 0], right, src)
        out(s, 1, ref, crv.at[s, 1], left, src)
        out(s, 2, ref, crv.at[s, 3], other, src)
        out(s, 3, ref, crv.at[s, 2], far, src)

    def bgo(s):
        ref = part(s, x, 1 - yh, col)
        take_all(ref, crv.at[s, 3])
        out(s, 4, ref, crv.at[s, 4], right)
        out(s, 5, ref, crv.at[s, 5], left)
        out(s, 6, ref, irv.at[s, 1], same)
        ref = part(s, xm, yh, col)
        take_all(ref, crv.at[s, 0])
        out(s, 7, ref, irv.at[s, 0], same)
        ref = part(s, xp, yh, col)
        take_all(ref, crv.at[s, 1])
        out(s, 8, ref, irv.at[s, 0], zp)
        ref = part(s, xo, yh, col)
        take_all(ref, crv.at[s, 2])
        out(s, 9, ref, crv.at[s, 6], other)
        out(s, 10, ref, irv.at[s, 0], zm)

    def ego(s):
        ref = part(s, xm, 1 - yh, col)
        take_all(ref, crv.at[s, 4])
        out(s, 11, ref, irv.at[s, 1], zp)
        ref = part(s, xp, 1 - yh, col)
        take_all(ref, crv.at[s, 5])
        out(s, 12, ref, irv.at[s, 1], zm)
        ref = part(s, xo, 1 - yh, col)
        take_all(ref, crv.at[s, 6])
        out(s, 13, ref, irv.at[s, 1], same)

    def hgo(s):
        _, W, cols = stage(s)
        take_all(W.at[pl.ds(0, 3), yh, c, 1 - col, :, cols], irv.at[s, 0])
        out(s, 14, W.at[:, yh, c, :, :, cols], srv.at[s, 0], sibling)

    def igo(s):
        _, W, cols = stage(s)
        take_all(W.at[:, 1 - yh, c, 1 - col, :, cols], irv.at[s, 1])
        out(s, 15, W.at[:, 1 - yh, c, :, :, cols], srv.at[s, 1], sibling)

    def whole(s):
        _, W, cols = stage(s)
        take_all(W.at[:, yh, 1 - c, :, :, cols], srv.at[s, 0])
        take_all(W.at[:, 1 - yh, 1 - c, :, :, cols], srv.at[s, 1])

    def compute(s):
        _, W, cols = stage(s)

        @pl.loop(0, cols.size // 256)
        def _(n):
            at = pl.ds(pl.multiple_of(cols.start + n * 256, 256), 256)
            w = W[:, :, :, :, :, at].reshape(-1, 256)
            if W is W1:
                v = dot(tok[...], w) + b_in[:, at]
                g = 0.5 * v * (1.0 + jnp.tanh(0.7978845608 * (v + 0.044715 * (v * v * v))))
                hid[:, at] = g.astype(BF16)
            else:
                summed[:, at] = tok[:, at].astype(F32) + dot(hid[...], w) + b_out[:, at]

    ago(0)
    ago(1)
    keep1 = pltpu.make_async_copy(win.at[c], W1.at[x, yh, c], loc.at[0])
    keep2 = pltpu.make_async_copy(wout.at[c], W2.at[x, yh, c], loc.at[1])
    keep1.start()
    keep2.start()

    for _, to in column:
        send(qf16.at[z], qf16.at[z], psend.at[0], zq.at[0], to)
        send(idsb.at[z], idsb.at[z], psend.at[1], zi.at[0], to)

    leaving.append((qf16.at[pl.ds(0, NZ - 1)], psend.at[0]))
    leaving.append((idsb.at[pl.ds(0, NZ - 1)], psend.at[1]))

    for j in range(4):
        selr[j] = pick(iota((128, 512), 1) == 4 * iota((128, 1), 0) + j)

    keep1.wait()
    keep2.wait()
    for copy in fetched[3:]:
        copy.wait()

    def prep_column():
        flat = qf16[...].reshape(NZ * 16, 256)
        for j in range(4):
            sel = pick(iota((64, 256), 1) == 4 * iota((64, 1), 0) + j)
            rows = dot(sel, flat).astype(BF16)
            qfs[2 * j] = rows[:, :128]
            qfs[2 * j + 1] = rows[:, 128:]
        qfr[f] = qfs[f]

    def prep_query():
        take_all(qf16.at[pl.ds(0, NZ - 1)], zq.at[0])
        flat = qf16[...].reshape(NZ * 16, 256)
        total_q = jnp.zeros((128, 1024), F32)
        m = iota((128, 1), 0)
        at = jnp.where(lo(m, 8) < 4, hi(m, 8) * 16 + lo(m, 8) * 4, -8)
        for j in range(4):
            sel = pick(iota((128, 256), 1) == at + j)
            rows = dot(sel, flat).astype(BF16)
            total_q = total_q + dot(rows, head[j * 256 : (j + 1) * 256, :])
        query[...] = total_q.astype(BF16)
        queryf[...] = query[...].astype(F32)


    def prep_count():
        take_all(idsb.at[pl.ds(0, NZ - 1)], zi.at[0])
        idst[...] = jnp.transpose(idsb[...].reshape(128, 128).astype(F32))
        pi = iota((128, 1), 0)
        pid = ((hi(pi, 64) * 32 + z * 2 + lo(hi(pi, 32), 2)) * NF + lo(hi(pi, 4), NF)) * 4 + lo(pi, 4)
        pid = pid.astype(F32)
        cT[...] = lax.fori_loop(
            0, 64,
            lambda t, a: a + (idst[pl.ds(t, 1), :] == pid).astype(F32),
            jnp.zeros((128, 128), F32),
        )


    extra = {3: prep_query}
    for tick in range(1, NS + 4):
        if tick <= NS:
            bgo(tick - 1)
            if tick + 1 < NS:
                ago(tick + 1)
        if 0 <= tick - 2 < NS:
            ego(tick - 2)
            hgo(tick - 2)
        if 0 <= tick - 3 < NS:
            igo(tick - 3)
        if tick in extra:
            extra[tick]()
        if 0 <= tick - 4 < NS:
            whole(tick - 4)
            compute(tick - 4)

    rows = []
    for i in range(4):
        v = summed[i * SEQ : (i + 1) * SEQ, :]
        center = v - jnp.mean(v, axis=-1, keepdims=True)
        spread_ = jnp.mean(center * center, axis=-1, keepdims=True)
        normed = center * lax.rsqrt(spread_ + eps)
        rows.append(jnp.sum(normed, axis=0, keepdims=True) * (1.0 / SEQ) * gain[...] + bias[...])
    pooled = jnp.concatenate(rows, axis=0)
    emb[...] = pooled.astype(BF16)
    r16[d] = spread(pooled)

    for to in plane:
        send(r16.at[d], r16.at[d], psend.at[4], rp.at[0], to)

    leaving.append((r16.at[pl.ds(0, NPLANE - 1)], psend.at[4]))

    prep_count()
    prep_column()
    lane = iota((1, 128), 1)
    mine = (hi(lane, 8) == z) & (lo(lane, 8) < 4)
    s_col = score_scale * jnp.sum(
        queryf[pl.ds(pl.multiple_of(z * 8, 8), 8), :] * posf[...], axis=-1, keepdims=True
    )
    s_pos = jnp.sum(
        jnp.where(iota((8, 128), 1) == z * 8 + iota((8, 128), 0), s_col, 0.0), axis=0, keepdims=True
    )

    take_all(r16.at[pl.ds(0, NPLANE - 1)], rp.at[0])
    flat_r = r16[...].reshape(NPLANE * 16, 256)
    s = jnp.zeros((128, 128), F32)
    for j in range(4):
        rows = dot(selr[j], flat_r).astype(BF16)
        rk[j] = rows
        s = s + dot(rows, query[:, j * 256 : (j + 1) * 256], (1, 1))
    s = s * score_scale
    count = cT[...]
    listed = count > 0.0
    high = jnp.max(jnp.where(listed, s, LOW), axis=0, keepdims=True)
    part = jnp.sum(
        jnp.where(listed, count * jnp.exp(jnp.where(listed, s - high, 0.0)), 0.0), axis=0, keepdims=True
    )
    high2 = jnp.where(mine, jnp.maximum(high, s_pos), high)
    part2 = part * jnp.exp(high - high2) + jnp.where(mine, jnp.exp(s_pos - high2), 0.0)
    r8 = iota((8, 128), 0)
    stb[z] = jnp.where(r8 == 0, high2, jnp.where(r8 == 1, part2, 0.0))

    for _, to in column:
        send(stb.at[z], stb.at[z], psend.at[5], zs.at[0], to)

    leaving.append((stb.at[pl.ds(0, NZ - 1)], psend.at[5]))

    for to in row:
        send(qfs.at[to], qfr.at[f], psend.at[2], fq.at[0], (dp, to))

    leaving.append((qfr.at[pl.ds(0, NF - 1)], psend.at[2]))

    for to in plane:
        send(pos16.at[d], pos16.at[d], psend.at[3], pp.at[0], to)

    leaving.append((pos16.at[pl.ds(0, NPLANE - 1)], psend.at[3]))

    j64 = iota((64, 1), 0)
    squeeze = pick(iota((64, 128), 1) == hi(j64, 4) * 8 + lo(j64, 4))

    take_all(stb.at[pl.ds(0, NZ - 1)], zs.at[0])
    stats = stb[...]
    highs, parts = stats[:, 0, :], stats[:, 1, :]
    top = jnp.max(highs, axis=0, keepdims=True)
    total = top + jnp.log(jnp.sum(parts * jnp.exp(highs - top), axis=0, keepdims=True))
    loss[...] = jnp.where(r8 == 0, jnp.where(mine, total - s_pos, 0.0), 0.0)
    coeff = jnp.where(mine, jnp.exp(jnp.where(mine, s_pos - total, 0.0)) - 1.0, 0.0)
    w = jnp.exp(jnp.where(listed, s - total, 0.0)).astype(BF16).astype(F32)
    w = jnp.where(listed, count * w, 0.0).astype(BF16)
    wr[f, 0:64, :] = dot(squeeze, w, (1, 1)).astype(BF16)
    c0 = coeff.astype(BF16).astype(F32)
    c1 = (coeff - c0).astype(BF16).astype(F32)
    c2 = coeff - c0 - c1
    r16i = iota((16, 128), 0)
    wr[f, 64:80, :] = jnp.where(
        r16i == 0, c0, jnp.where(r16i == 1, c1, jnp.where(r16i == 2, c2, 0.0))
    ).astype(BF16)

    for to in row:
        send(wr.at[f], wr.at[f], psend.at[6], fw.at[0], (dp, to))

    leaving.append((wr.at[pl.ds(0, NF - 1)], psend.at[6]))

    take_all(pos16.at[pl.ds(0, NPLANE - 1)], pp.at[0])
    flat_p = pos16[...].reshape(NPLANE * 16, 256)
    for j in range(4):
        pk[j] = dot(selr[j], flat_p).astype(BF16)
    take_all(qfr.at[pl.ds(0, NF - 1)], fq.at[0])
    slices = qfr[...].reshape(NF * 64, 128)
    e32, l32 = iota((32, 1), 0), iota((32, 128), 1)
    group_q = dot(pick(iota((32, 512), 1) == hi(e32, 4) * 64 + z * 4 + lo(e32, 4)), slices)
    expand = pick((hi(l32, 16) == hi(e32, 4)) & (lo(l32, 16) < 3))
    own_lane = l32 == z * 8 + lo(e32, 4)
    shift = pick(l32 == k * 32 + e32)

    take_all(wr.at[pl.ds(0, NF - 1)], fw.at[0])
    g_part = dot(slices, wr[:, 0:64, :].reshape(NF * 64, 128), (0, 0)).astype(BF16)
    co = dot(expand, wr[:, 64:80, :].reshape(128, 128))
    co = jnp.sum(jnp.where(own_lane, co, 0.0), axis=1, keepdims=True)
    g_pos = (group_q * co).astype(BF16)
    g_pos = dot(g_pos, shift, (0, 0)).astype(BF16)
    for e in range(4):
        gs[e, 0:32, :] = g_part[e * 32 : e * 32 + 32, :]
        gs[e, 32:64, :] = g_pos[e * 32 : e * 32 + 32, :]
    gr[k] = gs[k]

    for n, to in quarter:
        send(gs.at[n], gr.at[k], psend.at[7], gx.at[0], to)

    leaving.append((gr.at[pl.ds(0, 3)], psend.at[7]))

    take_all(gr.at[pl.ds(0, 3)], gx.at[0])
    g_all = jnp.sum(gr[...].astype(F32), axis=0).astype(BF16)
    for e in range(4):
        term = score_scale * (dot(g_all[0:32, :], rk[e]) + dot(g_all[32:64, :], pk[e]))
        term = term.astype(BF16)
        for t in range(4):
            rss[e * 2 + t % 2 + 8 * (t // 2)] = term[(t // 2) * 16 : (t // 2) * 16 + 16, (t % 2) * 128 : (t % 2) * 128 + 128]
    rsr[z] = rss[z]

    for n, to in column:
        send(rss.at[n], rsr.at[z], psend.at[8], zr.at[0], to)

    leaving.append((rsr.at[pl.ds(0, NZ - 1)], psend.at[8]))

    for copy in sent:
        copy.wait_send()
    early = len(leaving)
    for ref, sem in leaving:
        take_all(ref, sem)

    take_all(rsr.at[pl.ds(0, NZ - 1)], zr.at[0])
    agr[k, z] = jnp.sum(rsr[...].astype(F32), axis=0).astype(BF16)

    for _, to in column:
        send(agr.at[k, z], agr.at[k, z], psend.at[9], za.at[0], to)

    leaving.append((agr.at[0, pl.ds(0, NZ - 1)], psend.at[9]))

    take_all(agr.at[k, pl.ds(0, NZ - 1)], za.at[0])

    for _, to in quarter:
        send(agr.at[k], agr.at[k], psend.at[10], ga.at[0], to)

    leaving.append((agr.at[pl.ds(0, 3)], psend.at[10]))

    take_all(agr.at[pl.ds(0, 3)], ga.at[0])
    grads[...] = agr[...]

    for ref, sem in leaving[early:]:
        take_all(ref, sem)


def finish(emb_in, loss_in, parts, emb, loss, hg):
    z = rem(div(lax.axis_index("dp"), 2), NZ)
    emb[...] = emb_in[...]
    row, lane = loss_in[0:1, :], iota((1, 128), 1)
    for i in range(4):
        loss[i] = jnp.sum(jnp.where(lane == z * 8 + i, row, 0.0))
    for e in range(4):
        for t in range(NZ):
            row, at = e * 32 + (t // 8) * 16, (t % 8) * 128
            hg[row : row + 16, at : at + 128] = parts[e, t].astype(F32)


def body(
    tokens, w_in, b_in, w_out, b_out, ln_gain, ln_bias, head, query_feats, positive_rows, neg_ids
):
    vmem = pl.BlockSpec(memory_space=pltpu.VMEM)
    V, S = pltpu.VMEM, pltpu.SemaphoreType.DMA
    parts = pl.pallas_call(
        kernel,
        out_shape=(
            jax.ShapeDtypeStruct((4, 1024), BF16),
            jax.ShapeDtypeStruct((8, 128), F32),
            jax.ShapeDtypeStruct((4, NZ, 16, 128), BF16),
        ),
        in_specs=[pl.BlockSpec(memory_space=pl.ANY)] * 11,
        out_specs=(vmem,) * 3,
        scratch_shapes=[
            V((512, 1024), BF16),
            V((1, 2048), F32),
            V((1, 1024), F32),
            V((1, 1024), F32),
            V((1, 1024), F32),
            V((1024, 1024), BF16),
            V((4, 1024), BF16),
            V((4, 1024), BF16),
            V((4, 64), jnp.int32),
            S((9,)),
            V((4, 2, 2, 2, 32, 2048), BF16),
            V((4, 2, 2, 2, 64, 1024), BF16),
            V((512, 2048), BF16),
            V((512, 1024), F32),
            V((16, 256), F32),
            V((NZ, 16, 256), BF16),
            V((NZ, 8, 128), jnp.int32),
            V((NPLANE, 16, 256), BF16),
            V((NPLANE, 16, 256), BF16),
            V((NF, 64, 128), BF16),
            V((NF, 64, 128), BF16),
            V((128, 1024), BF16),
            V((128, 1024), F32),
            V((8, 1024), F32),
            V((128, 128), F32),
            V((128, 128), F32),
            V((4, 128, 256), BF16),
            V((4, 128, 256), BF16),
            V((4, 128, 512), BF16),
            V((NZ, 8, 128), F32),
            V((NF, 80, 128), BF16),
            V((4, 64, 128), BF16),
            V((4, 64, 128), BF16),
            V((NZ, 16, 128), BF16),
            V((NZ, 16, 128), BF16),
            V((4, NZ, 16, 128), BF16),
        ]
        + [S((NS, 7)), S((NS, 2)), S((NS, 2)), S((NS, 16)), S((2,))]
        + [S((1,))] * 11
        + [S((11,))],
        compiler_params=pltpu.CompilerParams(
            collective_id=0, has_side_effects=True, vmem_limit_bytes=60 << 20
        ),
    )(
        tokens,
        w_in.reshape(2, 2, 32, 2048),
        b_in.reshape(1, -1),
        w_out.reshape(2, 2, 64, 1024),
        b_out.reshape(1, -1),
        ln_gain.reshape(1, -1),
        ln_bias.reshape(1, -1),
        head,
        query_feats,
        positive_rows,
        neg_ids,
    )
    return pl.pallas_call(
        finish,
        out_shape=(
            jax.ShapeDtypeStruct((4, 1024), BF16),
            jax.ShapeDtypeStruct((4,), F32),
            jax.ShapeDtypeStruct((128, 1024), F32),
        ),
        in_specs=[vmem] * 3,
        out_specs=(vmem, pl.BlockSpec(memory_space=pltpu.SMEM), vmem),
    )(*parts)


def solution(mesh):
    in_specs = (
        P(("dp", "fsdp"), None),
        P("fsdp", None),
        P(),
        P("fsdp", None),
        P(),
        P(),
        P(),
        P(),
        P(("dp", "fsdp"), None),
        P(("dp", "fsdp"), None),
        P(("dp", "fsdp"), None),
    )
    out_specs = (P(("dp", "fsdp"), None), P(("dp", "fsdp")), P("fsdp", None))
    return jax.shard_map(body, mesh=mesh, in_specs=in_specs, out_specs=out_specs, check_vma=False)
```
